32 devices in a mesh: lon: 8 (over y, x, core), lat: 4 (over z).
Axes of the slice: x: 2, y: 2, z: 4, core: 2. Of those that a mesh axis runs over, the one named last changes fastest.
Arguments:
- vel_base: bfloat16 [8, 4, 8, 16, 2, 128], P('lon', 'lat'), may hold values from -1.25 to 1.25
- vel_grad: bfloat16 [8, 4, 8, 16, 4, 128], P('lon', 'lat'), may hold values from -0.29882812 to 0.29882812
- route_dev: int32 [8, 4, 8, 128, 1], P('lon', 'lat'), may hold values from 0 to 31; in each aligned block of 128 rows (0 to 127, 128 to 255, ..., all dimensions but the last counted through in order) at most 8 rows name the same one
- route_block: int32 [8, 4, 8, 128], P('lon', 'lat'), may hold values from 0 to 15
- seed_cells: int32 [8, 2048, 1024], P(None, 'lat', 'lon'), may hold values from 0 to 127
Outputs:
- flow_map: float32 [2, 2048, 1024], P(None, 'lat', 'lon')
- ftle_field: float32 [2048, 1024], P('lat', 'lon')
The draws below stay inside these ranges and needn't reach their ends.
Inputs may be any that keep to these rules, and one draw needn't show every extreme that they name: `route_dev`: in each step, at most 8 of the 128 seed groups of one device name the same owner; in some steps of some devices an owner is named by exactly 8 groups.
All inputs are finite; a program needn't handle non-finite values.
Results may differ from the reference program's by a relative error of at most 0.0003.
Values may be sent and summed in bfloat16 or wider, within the bound.
No kernel may reach another device: no remote copies, remote signals or barrier semaphores. Data moves between devices by JAX's collectives and lax.ppermute only.
A program may use at most 64 MiB of HBM per device.

```python
import math
import jax
import jax.numpy as jnp
import numpy as np

SEED_LAT = 512
SEED_LON = 128
GROUP_ROWS = 4
CELLS_PER_BLOCK = 128
BLOCKS_DEV = 16
STEPS = 8
GROUPS = 128
SLOTS = 8
GRID_LAT = 2048
GRID_LON = 1024
N_LON = 8
N_LAT = 4
DEVICES = 32


def set_ends(result, stream_key, low, high):
    shape = result.shape
    index_at = [jax.random.randint(jax.random.fold_in(stream_key, axis), (), 0, shape[axis]) for axis in range(len(shape))]
    result = result.at[tuple(index_at)].set(low)
    longest = shape.index(max(shape))
    index_at[longest] = (index_at[longest] + 1) % shape[longest]
    return result.at[tuple(index_at)].set(high)


def block_scale(rng, extent, pieces, smallest, top_value):
    gain, own = 1.0, jax.random.fold_in(rng, 6)
    for dim, shards_of in pieces:
        draws = jnp.exp(jax.random.uniform(jax.random.fold_in(own, dim), (shards_of,), jnp.float32, smallest / len(pieces), top_value / len(pieces)))
        gain = gain * jnp.repeat(draws, extent[dim] // shards_of).reshape([-1 if axis == dim else 1 for axis in range(len(extent))])
    return gain


def routed_block(rng, own, number, rows, number_of, top, most, slope):
    sequence = jax.random.permutation(rng, number_of)
    heavy_load, usual = load_shares(number_of, rows * top, most, slope, True), load_shares(number_of, rows * top, most, slope, False)
    places = jnp.arange(number_of)

    def named(lengths, turn):
        used = int((lengths > 0).sum())
        fixed = max(1, used // 4)
        moved = fixed + (places - fixed + turn * (used - fixed)) % max(1, number_of - fixed)
        return jnp.zeros((number_of,), jnp.int32).at[sequence[jnp.where(places < fixed, places, moved)]].set(jnp.asarray(lengths, jnp.int32))

    lengths = jnp.where(number % 4 == 0, named(heavy_load, number // 4), named(usual, number - number // 4 - 1))
    mixed = jax.random.permutation(jax.random.fold_in(own, 3), number_of)
    source_of, sink = mixed[0:number_of // 2 * 2:2], mixed[1:number_of // 2 * 2:2]
    room = jnp.minimum(lengths[source_of] - 1, most - lengths[sink]) // 2
    room = jnp.where((source_of == sequence[0]) | (sink == sequence[0]) | (lengths[sink] == 0), 0, jnp.maximum(room, 0))
    moved = jax.random.randint(jax.random.fold_in(own, 4), (number_of // 2,), 0, 1 << 20) % (room + 1)
    lengths = lengths.at[source_of].add(-moved).at[sink].add(moved)
    items = jnp.searchsorted(jnp.cumsum(lengths), jnp.arange(rows * top), side="right").astype(jnp.int32)
    grid = items.reshape(top, rows).T
    grid = grid[jax.random.permutation(jax.random.fold_in(own, 1), rows)]
    turn = jax.random.randint(jax.random.fold_in(own, 2), (rows, 1), 0, top)
    return jnp.take_along_axis(grid, (jnp.arange(top)[None, :] + turn) % top, axis=1)


def load_shares(number_of, total, most, lean, full):
    loads = [(1 << 20) // math.isqrt(standing ** lean) + 1 for standing in range(1, number_of + 1)]
    largest = most if full else min(most, max(-(-total // number_of), total * loads[0] // sum(loads)))
    least = 1 if total - largest >= number_of - 1 else 0
    given, rest = [largest] + [least] * (number_of - 1), total - largest - least * (number_of - 1)
    while rest > 0:
        movable = [i for i in range(1, number_of) if given[i] < largest] or [i for i in range(1, number_of) if given[i] < most]
        mass, budget = sum([loads[i] for i in movable]), rest
        for i in movable:
            more = min(most - given[i], max(1, budget * loads[i] // mass), rest)
            given[i] = given[i] + more
            rest = rest - more
    return np.array(given)


def centred(own_key, dims, width, bound, cuts=(), dtype=jnp.bfloat16):
    level = block_scale(own_key, dims, cuts, -0.22, 0.18) if cuts else 1.0
    result = jax.random.normal(own_key, dims, jnp.float32) * width * level
    return jnp.minimum(jnp.maximum(result, -bound), bound).astype(dtype)


def setup_inputs(seed: int = 0) -> dict:
    key_of = jax.random.split(jax.random.key(seed), 6)
    vel_base = centred(key_of[0], (N_LON, N_LAT, STEPS, BLOCKS_DEV, 2, CELLS_PER_BLOCK), 0.09, 1.25, ((0, 8), (1, 4)))
    vel_grad = jnp.clip(jax.random.uniform(key_of[1], (N_LON, N_LAT, STEPS, BLOCKS_DEV, 4, CELLS_PER_BLOCK), jnp.float32, -0.29882812, 0.29882812) * block_scale(key_of[1], (N_LON, N_LAT, STEPS, BLOCKS_DEV, 4, CELLS_PER_BLOCK), ((0, 8), (1, 4)), -0.4, 0.0), -0.29882812, 0.29882812).astype(jnp.bfloat16)
    route_dev_keys = jax.random.split(jax.random.fold_in(key_of[2], 1), N_LON * N_LAT * STEPS * GROUPS // GROUPS)
    route_dev_turns = jax.random.permutation(jax.random.fold_in(key_of[2], 3), N_LON * N_LAT * STEPS * GROUPS // GROUPS)
    route_dev = jax.vmap(lambda own, number: routed_block(jax.random.fold_in(key_of[2], 2), own, number, GROUPS, DEVICES, 1, SLOTS, 2))(route_dev_keys, route_dev_turns).reshape((N_LON, N_LAT, STEPS, GROUPS, 1))
    route_block = set_ends(jax.random.randint(key_of[3], (N_LON, N_LAT, STEPS, GROUPS), 0, BLOCKS_DEV), jax.random.fold_in(key_of[3], 1), 0, BLOCKS_DEV - 1).astype(jnp.int32)
    seed_cells = set_ends(jax.random.randint(key_of[4], (STEPS, GRID_LAT, GRID_LON), 0, CELLS_PER_BLOCK), jax.random.fold_in(key_of[4], 1), 0, CELLS_PER_BLOCK - 1).astype(jnp.int32)
    return {"vel_base": vel_base, "vel_grad": vel_grad, "route_dev": route_dev, "route_block": route_block, "seed_cells": seed_cells}


def velocity_rate(eastward_component, along_y, coeffs):
    vel_x, vel_y, grad_xx, grad_xy, grad_yx, grad_yy = coeffs
    return (-(vel_x + grad_xx * eastward_component + grad_xy * along_y), -(vel_y + grad_yx * eastward_component + grad_yy * along_y))

def runge_kutta(eastward_component, along_y, coeffs, dt_step):
    half_step = 0.5 * dt_step
    rate_one = velocity_rate(eastward_component, along_y, coeffs)
    rate_two = velocity_rate(eastward_component + half_step * rate_one[0], along_y + half_step * rate_one[1], coeffs)
    rate_three = velocity_rate(eastward_component + half_step * rate_two[0], along_y + half_step * rate_two[1], coeffs)
    rate_four = velocity_rate(eastward_component + dt_step * rate_three[0], along_y + dt_step * rate_three[1], coeffs)
    sixth = dt_step / 6.0
    new_x = eastward_component + sixth * (rate_one[0] + 2.0 * rate_two[0] + 2.0 * rate_three[0] + rate_four[0])
    new_y = along_y + sixth * (rate_one[1] + 2.0 * rate_two[1] + 2.0 * rate_three[1] + rate_four[1])
    return (new_x, new_y)

def stretch_rate(diff_lon, diff_lat):
    map_xx = 1.0 + diff_lon[0]
    map_xy = diff_lat[0]
    map_yx = diff_lon[1]
    map_yy = 1.0 + diff_lat[1]
    green_xx = map_xx * map_xx + map_yx * map_yx
    green_yy = map_xy * map_xy + map_yy * map_yy
    green_xy = map_xx * map_xy + map_yx * map_yy
    half_diff = 0.5 * (green_xx - green_yy)
    largest = 0.5 * (green_xx + green_yy) + jnp.sqrt(half_diff * half_diff + green_xy * green_xy)
    return 0.5 * jnp.log(largest)

def arrange(route_table):
    lat_groups = SEED_LAT // GROUP_ROWS
    lon_groups = SEED_LON // 128
    shaped = route_table.reshape(N_LON, N_LAT, STEPS, lat_groups, lon_groups)
    shaped = jnp.transpose(shaped, (2, 1, 3, 0, 4))
    return shaped.reshape(STEPS, N_LAT * lat_groups, N_LON * lon_groups)

def reference(vel_base, vel_grad, route_dev, route_block, seed_cells):
    owners = arrange(route_dev[..., 0]).astype(jnp.int32)
    blocks = arrange(route_block).astype(jnp.int32)
    vel_table = jnp.concatenate([vel_base, vel_grad], axis=4).reshape(-1)
    dt_step = 1.0 / STEPS
    eastward_component = jnp.zeros((GRID_LAT, GRID_LON), jnp.float32)
    along_y = jnp.zeros((GRID_LAT, GRID_LON), jnp.float32)
    for step_index in range(STEPS):
        block_id = (owners[step_index] * STEPS + step_index) * BLOCKS_DEV + blocks[step_index]
        block_id = jnp.repeat(jnp.repeat(block_id, GROUP_ROWS, axis=0), 128, axis=1)
        offset = (block_id * (6 * CELLS_PER_BLOCK) + seed_cells[step_index]).astype(jnp.int32)
        coeffs = tuple((jnp.take(vel_table, offset + component * CELLS_PER_BLOCK).astype(jnp.float32) for component in range(6)))
        eastward_component, along_y = runge_kutta(eastward_component, along_y, coeffs, dt_step)
    flow_map = jnp.stack([eastward_component, along_y])
    diff_lon = (jnp.roll(flow_map, -1, axis=2) - jnp.roll(flow_map, 1, axis=2)) * 0.5
    padded = jnp.pad(flow_map, ((0, 0), (1, 1), (0, 0)), mode='edge')
    diff_lat = (padded[:, 2:] - padded[:, :-2]) * 0.5
    return (flow_map, stretch_rate(diff_lon, diff_lat))
```

```python
import functools

import jax
import jax.numpy as jnp
from jax import lax
from jax.experimental import pallas as pl
from jax.experimental.pallas import tpu as pltpu
from jax.sharding import PartitionSpec as P

GROUP_ROWS = 4
LANES = 128
SPLIT = 4


def swap(value, axis, masks):
    count = lax.axis_size(axis)
    pairs = [(i, i ^ masks[i % len(masks)]) for i in range(count)]
    return lax.ppermute(value, axis, pairs)


def plane_masks(n_lon):
    bits = []
    mask = 2
    while mask < n_lon:
        bits.append(mask)
        mask *= 2
    return bits, bits[::-1]


def plane_gather(shard):
    even, odd = plane_masks(lax.axis_size("lon"))
    held = shard[None]
    for even_mask, odd_mask in zip(even, odd):
        held = jnp.concatenate([held, swap(held, "lon", (even_mask, odd_mask))], axis=0)
    return held


def slot_of(owners, n_lat):
    lon, lat = lax.axis_index("lon"), lax.axis_index("lat")
    even, odd = plane_masks(lax.axis_size("lon"))
    owner_lon, owner_lat = owners // n_lat, owners % n_lat
    family = (owner_lon ^ lon) & 1
    base = lon ^ family
    parity = base & 1
    apart = owner_lon ^ base
    place = jnp.zeros_like(owners)
    for position, (even_mask, odd_mask) in enumerate(zip(even, odd)):
        mask = jnp.where(parity == 0, even_mask, odd_mask)
        place = place + jnp.where((apart & mask) != 0, 1 << position, 0)
    return (family * n_lat + (owner_lat ^ lat)) * (1 << len(even)) + place


def advance(along_x, along_y, coeffs):
    vel_x, vel_y, xx, xy, yx, yy = coeffs
    half_x = vel_x + xx * along_x + xy * along_y
    half_y = vel_y + yx * along_x + yy * along_y
    full_x = half_x + half_x
    full_y = half_y + half_y
    third_x = full_x + (xx * half_x + xy * half_y)
    third_y = full_y + (yx * half_x + yy * half_y)
    ratio = 2.0 / 3.0
    second_x = full_x + ratio * (xx * third_x + xy * third_y)
    second_y = full_y + ratio * (yx * third_x + yy * third_y)
    new_x = along_x + (full_x + (xx * second_x + xy * second_y))
    new_y = along_y + (full_y + (yx * second_x + yy * second_y))
    return new_x, new_y


def steps_kernel(first, scale, piece_steps, n_pieces, has_start, unroll, *refs):
    base_ref, grad_ref, cells_ref = refs[:3]
    pieces = refs[3 : 3 + n_pieces]
    start_ref = refs[3 + n_pieces] if has_start else None
    out_ref, table = refs[-2:]
    steps, rows, lanes = cells_ref.shape
    places, _, step_rows, _ = pieces[0].shape
    for number, piece in enumerate(pieces):

        def widen(place, carry, number=number, piece=piece):
            for step in range(steps):
                row = ((number * places + place) * steps + step) * step_rows
                row = pl.multiple_of(row, step_rows)
                source = piece[place, piece_steps[number] + step]
                table[pl.ds(row, step_rows), :] = source.astype(jnp.float32) * scale
            return carry

        lax.fori_loop(0, places, widen, 0)
    upper = lax.broadcasted_iota(jnp.int32, (8, lanes), 0) < GROUP_ROWS

    def tile(number):
        row = pl.multiple_of(number * 8, 8)
        if has_start:
            along_x = start_ref[0, pl.ds(row, 8), :]
            along_y = start_ref[1, pl.ds(row, 8), :]
        else:
            along_x = jnp.zeros((8, lanes), jnp.float32)
            along_y = jnp.zeros((8, lanes), jnp.float32)
        for step in range(steps):
            index = cells_ref[step, pl.ds(row, 8), :]
            one, two = 2 * number, 2 * number + 1
            sources = [
                (base_ref[first + step, one] + k, base_ref[first + step, two] + k) for k in range(2)
            ]
            sources += [
                (grad_ref[first + step, one] + k, grad_ref[first + step, two] + k) for k in range(4)
            ]
            coeffs = []
            for above, below in sources:
                values = jnp.where(
                    upper,
                    jnp.broadcast_to(table[pl.ds(above, 1), :], (8, lanes)),
                    jnp.broadcast_to(table[pl.ds(below, 1), :], (8, lanes)),
                )
                coeffs.append(
                    jnp.take_along_axis(values, index, axis=1, mode="promise_in_bounds")
                )
            along_x, along_y = advance(along_x, along_y, coeffs)
        out_ref[0, pl.ds(row, 8), :] = along_x
        out_ref[1, pl.ds(row, 8), :] = along_y

    def tiles(number, carry):
        for inner in range(unroll):
            tile(number * unroll + inner)
        return carry

    lax.fori_loop(0, rows // 8 // unroll, tiles, 0)


def run_steps(first, last, scale, base, grad, cells, pieces, piece_steps, start):
    steps = last - first
    _, rows, lanes = cells.shape
    places, _, step_rows, _ = pieces[0].shape
    table_rows = len(pieces) * places * steps * step_rows
    vmem = pl.BlockSpec(memory_space=pltpu.VMEM)
    smem = pl.BlockSpec(memory_space=pltpu.SMEM)
    operands = [base, grad, cells[first:last], *pieces] + ([start] if start is not None else [])
    need = table_rows * lanes * 4 + sum(value.size * value.dtype.itemsize for value in operands)
    need += 2 * rows * lanes * 4
    return pl.pallas_call(
        functools.partial(
            steps_kernel, first, scale, piece_steps, len(pieces), start is not None, 8
        ),
        out_shape=jax.ShapeDtypeStruct((2, rows, lanes), jnp.float32),
        in_specs=[smem, smem] + [vmem] * (len(operands) - 2),
        out_specs=vmem,
        scratch_shapes=[pltpu.VMEM((table_rows, lanes), jnp.float32)],
        compiler_params=pltpu.CompilerParams(vmem_limit_bytes=need + (4 << 20)),
        name=f"rk_steps_{first}",
    )(*operands)


def stretch_rate(diff_lon, diff_lat):
    map_xx = 1.0 + diff_lon[0]
    map_xy = diff_lat[0]
    map_yx = diff_lon[1]
    map_yy = 1.0 + diff_lat[1]
    green_xx = map_xx * map_xx + map_yx * map_yx
    green_yy = map_xy * map_xy + map_yy * map_yy
    green_xy = map_xx * map_xy + map_yx * map_yy
    half_diff = 0.5 * (green_xx - green_yy)
    largest = 0.5 * (green_xx + green_yy) + jnp.sqrt(half_diff * half_diff + green_xy * green_xy)
    return 0.5 * jnp.log(largest)


def shifted(value, axis, by):
    count = lax.axis_size(axis)
    return lax.ppermute(value, axis, [(i, (i + by) % count) for i in range(count)])


def body(vel_base, vel_grad, route_dev, route_block, seed_cells):
    n_lon, n_lat = lax.axis_size("lon"), lax.axis_size("lat")
    num_steps, rows, lanes = seed_cells.shape
    blocks = vel_base.shape[3]
    shard = jnp.concatenate(
        [
            vel_base.reshape(num_steps, 2 * blocks, lanes),
            vel_grad.reshape(num_steps, 4 * blocks, lanes),
        ],
        axis=1,
    )
    step_rows = shard.shape[1]
    spans = [(0, SPLIT), (SPLIT, num_steps)]
    rounds = []
    for apart in range(n_lat):
        if apart < n_lat - 1:
            parts = [(0, num_steps)]
        else:
            parts = spans
        for begin, end in parts:
            piece = shard[begin:end]
            if apart:
                piece = swap(piece, "lat", (apart,))
            mine = plane_gather(piece)
            other = swap(mine, "lon", (1,))
            rounds.append((apart, begin, end, mine, other))
    owners = route_dev[0, 0, :, :, 0]
    slots = slot_of(owners, n_lat)
    scale = -0.5 / num_steps
    flow = None
    for first, last in spans:
        chosen = [item for item in rounds if item[1] <= first and last <= item[2]]
        pieces = [item[3] for item in chosen] + [item[4] for item in chosen]
        piece_steps = tuple([first - item[1] for item in chosen] * 2)
        local = jnp.arange(num_steps, dtype=jnp.int32)[:, None] - first
        row = (slots * (last - first) + local) * step_rows
        base = row + 2 * route_block[0, 0]
        grad = row + 2 * blocks + 4 * route_block[0, 0]
        flow = run_steps(
            first, last, scale, base, grad, seed_cells, pieces, piece_steps, flow
        )
    west = shifted(flow[:, :, -1], "lon", 1)
    east = shifted(flow[:, :, 0], "lon", -1)
    south = shifted(flow[:, -1:, :], "lat", 1)
    north = shifted(flow[:, :1, :], "lat", -1)
    lat_index = lax.axis_index("lat")
    south = jnp.where(lat_index == 0, flow[:, :1, :], south)
    north = jnp.where(lat_index == n_lat - 1, flow[:, -1:, :], north)
    right = jnp.concatenate([flow[:, :, 1:], east[:, :, None]], axis=2)
    left = jnp.concatenate([west[:, :, None], flow[:, :, :-1]], axis=2)
    diff_lon = (right - left) * 0.5
    lat_rows = jnp.concatenate([south, flow, north], axis=1)
    diff_lat = (lat_rows[:, 2:] - lat_rows[:, :-2]) * 0.5
    return (flow, stretch_rate(diff_lon, diff_lat))


def solution(mesh):
    in_specs = (
        P("lon", "lat", None, None, None, None),
        P("lon", "lat", None, None, None, None),
        P("lon", "lat", None, None, None),
        P("lon", "lat", None, None),
        P(None, "lat", "lon"),
    )
    out_specs = (P(None, "lat", "lon"), P("lat", "lon"))
    return jax.shard_map(body, mesh=mesh, in_specs=in_specs, out_specs=out_specs, check_vma=False)
```

```python
import functools

import jax
import jax.numpy as jnp
from jax import lax
from jax.experimental import pallas as pl
from jax.experimental.pallas import tpu as pltpu
from jax.sharding import PartitionSpec as P

GROUP_ROWS = 4
TABLE_BYTES = 13 << 20
WAITS = {
    "z3": ("z1",),
    "edge": ("r0.1",),
    "r1.1": ("z1",),
    "r2.1": ("z1",),
    "r1.2": ("r0.2",),
    "c2": ("r3.1",),
}


def after(value, *earlier):
    return lax.optimization_barrier((value, *earlier))[0] if earlier else value


def swap(value, axis, masks):
    count = lax.axis_size(axis)
    pairs = [(i, i ^ masks[i % len(masks)]) for i in range(count)]
    return lax.ppermute(value, axis, pairs)


def plane_masks(n_lon):
    bits = []
    mask = 2
    while mask < n_lon:
        bits.append(mask)
        mask *= 2
    return bits, bits[::-1]


def slot_of(owners, n_lat):
    lon, lat = lax.axis_index("lon"), lax.axis_index("lat")
    even, odd = plane_masks(lax.axis_size("lon"))
    places = 1 << len(even)
    owner_lon, owner_lat = owners // n_lat, owners % n_lat
    apart = owner_lat ^ lat
    foreign = (owner_lon ^ lon) & 1
    base = lon ^ foreign
    diff = owner_lon ^ base
    place = jnp.zeros_like(owners)
    for position, (even_mask, odd_mask) in enumerate(zip(even, odd)):
        mask = jnp.where((base & 1) == 0, even_mask, odd_mask)
        place = place + jnp.where((diff & mask) != 0, 1 << position, 0)
    return (apart * 2 + foreign) * places + place


def advance(along_x, along_y, coeffs):
    vel_x, vel_y, xx, xy, yx, yy = coeffs
    half_x = vel_x + xx * along_x + xy * along_y
    half_y = vel_y + yx * along_x + yy * along_y
    full_x = half_x + half_x
    full_y = half_y + half_y
    third_x = full_x + (xx * half_x + xy * half_y)
    third_y = full_y + (yx * half_x + yy * half_y)
    ratio = 2.0 / 3.0
    second_x = full_x + ratio * (xx * third_x + xy * third_y)
    second_y = full_y + ratio * (yx * third_x + yy * third_y)
    new_x = along_x + (full_x + (xx * second_x + xy * second_y))
    new_y = along_y + (full_y + (yx * second_x + yy * second_y))
    return new_x, new_y


def steps_kernel(first, scale, step_rows, slots, has_start, last, unroll, *refs):
    count = len(slots)
    base_ref, grad_ref, edge_ref, cells_hbm = refs[:4]
    pieces = refs[4 : 4 + count]
    start_ref, start_edge = refs[4 + count : 6 + count] if has_start else (None, None)
    rest = refs[(6 if has_start else 4) + count :]
    flow_ref, out_edge, table, cells_ref, arrived = rest[0], rest[1], *rest[-3:]
    out_ref, out_sides = rest[2:4] if last else (None, None)
    steps, rows, lanes = cells_ref.shape
    fetch = pltpu.make_async_copy(cells_hbm.at[pl.ds(first, steps)], cells_ref, arrived)
    fetch.start()
    for slot, piece in zip(slots, pieces):

        def widen(part, carry, slot=slot, piece=piece):
            place, step = part // steps, part % steps
            source = pl.multiple_of((first + step) * step_rows, step_rows)
            row = pl.multiple_of((slot * steps + part) * step_rows, step_rows)
            values = piece[place, pl.ds(source, step_rows), :].astype(jnp.float32) * scale
            table[pl.ds(row, step_rows), :] = values
            return carry

        lax.fori_loop(0, piece.shape[0] * steps, widen, 0, unroll=4)
    fetch.wait()
    upper = lax.broadcasted_iota(jnp.int32, (8, lanes), 0) < GROUP_ROWS
    lane = lax.broadcasted_iota(jnp.int32, (8, lanes), 1)
    zero = jnp.zeros((8, lanes), jnp.float32)

    def begin_at(ref, row):
        return (ref[0, pl.ds(row, 8), :], ref[1, pl.ds(row, 8), :]) if has_start else (zero, zero)

    def tile(one, two, indices, along_x, along_y):
        for step in range(steps):
            index = indices(step)
            sources = [
                (ref[first + step, one] + k, ref[first + step, two] + k)
                for ref, number in ((base_ref, 2), (grad_ref, 4))
                for k in range(number)
            ]
            coeffs = []
            for above, below in sources:
                values = jnp.where(
                    upper,
                    jnp.broadcast_to(table[pl.ds(above, 1), :], (8, lanes)),
                    jnp.broadcast_to(table[pl.ds(below, 1), :], (8, lanes)),
                )
                coeffs.append(
                    jnp.take_along_axis(values, index, axis=1, mode="promise_in_bounds")
                )
            along_x, along_y = advance(along_x, along_y, coeffs)
        return along_x, along_y

    def tiles(number, carry):
        for inner in range(unroll):
            at = number * unroll + inner
            row = pl.multiple_of(at * 8, 8)
            start = begin_at(start_ref, row)
            end = tile(2 * at, 2 * at + 1, lambda step: cells_ref[step, pl.ds(row, 8), :], *start)
            if last:
                out_ref[0, pl.ds(row, 8), :], out_ref[1, pl.ds(row, 8), :] = end
            flow_ref[0, pl.ds(row, 8), :], flow_ref[1, pl.ds(row, 8), :] = end
        return carry

    lax.fori_loop(0, rows // 8 // unroll, tiles, 0)
    groups = rows // GROUP_ROWS
    start = begin_at(start_edge, 0)
    end = tile(groups, groups + 1, lambda step: edge_ref[first + step], *start)
    out_edge[0], out_edge[1] = end
    if not last:
        return
    half = lanes // 2
    ends = jnp.where(lane < half, 0, lanes - 1)
    for part in range(2):
        sides = [zero] * 4
        for at in range(rows // 8):
            value = flow_ref[part, at * 8 : at * 8 + 8, :]
            value = jnp.take_along_axis(value, ends, axis=1, mode="promise_in_bounds")
            sides[at % 4] = jnp.where((lane & (half - 1)) == at, value, sides[at % 4])
        out_sides[part] = (sides[0] + sides[1]) + (sides[2] + sides[3])


def run_steps(first, last, scale, step_rows, base, grad, edge_cells, cells, items, start):
    num_steps, rows, lanes = cells.shape
    steps = last - first
    pieces = [item[0] for item in items]
    slots = tuple(item[1] for item in items)
    height = sum(piece.shape[0] for piece in pieces) * steps * step_rows
    vmem = pl.BlockSpec(memory_space=pltpu.VMEM)
    smem = pl.BlockSpec(memory_space=pltpu.SMEM)
    need = height * lanes * 4 + steps * rows * lanes * 4
    small = jax.ShapeDtypeStruct((2, 8, lanes), jnp.float32)
    whole = jax.ShapeDtypeStruct((2, rows, lanes), jnp.float32)
    final = last == num_steps
    starts = list(start) if first else []
    return pl.pallas_call(
        functools.partial(steps_kernel, first, scale, step_rows, slots, first > 0, final, 8),
        out_shape=(whole, small) + ((whole, small) if final else ()),
        in_specs=[smem, smem, vmem, pl.BlockSpec(memory_space=pltpu.HBM)] + [vmem] * len(pieces + starts),
        out_specs=(vmem,) * (4 if final else 2),
        scratch_shapes=[
            pltpu.VMEM((height, lanes), jnp.float32),
            pltpu.VMEM((steps, rows, lanes), jnp.int32),
            pltpu.SemaphoreType.DMA(()),
        ],
        cost_estimate=pl.CostEstimate(
            flops=40 * steps * rows * lanes, bytes_accessed=16 << 20, transcendentals=0
        ),
        compiler_params=pltpu.CompilerParams(vmem_limit_bytes=need + (3 << 20)),
        name=f"rk_steps_{first}",
    )(base, grad, edge_cells, cells, *pieces, *starts)


def stretch_kernel(flag_ref, flow_ref, edge_ref, inner_ref, outer_ref, out_ref):
    _, rows, lanes = flow_ref.shape
    half = lanes // 2
    lane = lax.broadcasted_iota(jnp.int32, (8, lanes), 1)
    row = lax.broadcasted_iota(jnp.int32, (8, lanes), 0)
    odd, lowest, highest = flag_ref[0] == 1, flag_ref[1] == 1, flag_ref[2] == 1
    sides, south, north = [], [], []
    for part in range(2):
        inner, outer = inner_ref[part], outer_ref[part]
        west, east = jnp.where(odd, inner, outer), jnp.where(odd, outer, inner)
        sides.append(jnp.where(lane < half, east, west))
        south.append(jnp.where(lowest, flow_ref[part, 0:1, :], edge_ref[part, 0:1, :]))
        beyond = edge_ref[part, GROUP_ROWS : GROUP_ROWS + 1, :]
        north.append(jnp.where(highest, flow_ref[part, rows - 1 : rows, :], beyond))
    tiles = rows // 8
    for at in range(tiles):
        start = at * 8
        index = jnp.where(lane < half, half + at, at)
        diff_lon, diff_lat = [], []
        for part in range(2):
            flow = flow_ref[part, start : start + 8, :]
            halo = jnp.take_along_axis(sides[part], index, axis=1, mode="promise_in_bounds")
            left = jnp.where(lane == 0, halo, pltpu.roll(flow, 1, 1))
            right = jnp.where(lane == lanes - 1, halo, pltpu.roll(flow, lanes - 1, 1))
            diff_lon.append((right - left) * 0.5)
            under = south[part] if at == 0 else flow_ref[part, start - 1 : start, :]
            over = north[part] if at == tiles - 1 else flow_ref[part, start + 8 : start + 9, :]
            below = jnp.where(row == 0, jnp.broadcast_to(under, flow.shape), pltpu.roll(flow, 1, 0))
            above = jnp.where(row == 7, jnp.broadcast_to(over, flow.shape), pltpu.roll(flow, 7, 0))
            diff_lat.append((above - below) * 0.5)
        out_ref[start : start + 8, :] = stretch_rate(diff_lon, diff_lat)


def stretch_rate(diff_lon, diff_lat):
    map_xx = 1.0 + diff_lon[0]
    map_xy = diff_lat[0]
    map_yx = diff_lon[1]
    map_yy = 1.0 + diff_lat[1]
    green_xx = map_xx * map_xx + map_yx * map_yx
    green_yy = map_xy * map_xy + map_yy * map_yy
    green_xy = map_xx * map_xy + map_yx * map_yy
    half_diff = 0.5 * (green_xx - green_yy)
    largest = 0.5 * (green_xx + green_yy) + jnp.sqrt(half_diff * half_diff + green_xy * green_xy)
    return 0.5 * jnp.log(largest)


def body(vel_base, vel_grad, route_dev, route_block, seed_cells):
    n_lon, n_lat = lax.axis_size("lon"), lax.axis_size("lat")
    num_steps, rows, lanes = seed_cells.shape
    blocks = vel_base.shape[3]
    step_rows = 6 * blocks
    shard = jnp.concatenate(
        [
            vel_base.reshape(num_steps, 2 * blocks, lanes),
            vel_grad.reshape(num_steps, 4 * blocks, lanes),
        ],
        axis=1,
    ).reshape(num_steps * step_rows, lanes)
    places = n_lon // 2
    owners = route_dev[0, 0, :, :, 0]
    wanted = route_block[0, 0]
    done = {}

    def gated(value, label):
        return after(value, *[done[name] for name in WAITS.get(label, ())])

    came = [shard]
    for apart in range(1, n_lat):
        done[f"z{apart}"] = swap(gated(shard, f"z{apart}"), "lat", (apart,))
        came.append(done[f"z{apart}"])
    even, odd = plane_masks(n_lon)
    held = [value[None] for value in came]
    for stage, masks in enumerate(zip(even, odd)):
        for apart in range(n_lat):
            label = f"r{apart}.{stage + 1}"
            sent = gated(held[apart], label)
            done[label] = swap(sent, "lon", masks)
            held[apart] = jnp.concatenate([sent, done[label]])
    items = []
    for apart in range(n_lat):
        other = swap(gated(held[apart], f"c{apart}"), "lon", (1,))
        items += [(held[apart], 2 * apart * places), (other, (2 * apart + 1) * places)]

    def edge_of(row):
        value = jnp.stack([seed_cells[:, row, :], owners, wanted])
        return gated(value, "edge")

    south = lax.ppermute(edge_of(-1), "lat", [(i, i + 1) for i in range(n_lat - 1)])
    north = lax.ppermute(edge_of(0), "lat", [(i + 1, i) for i in range(n_lat - 1)])
    edge_cells = jnp.repeat(jnp.stack([south[0], north[0]], axis=1), GROUP_ROWS, axis=1)
    owners = jnp.concatenate([owners, south[1, :, -1:], north[1, :, :1]], axis=1)
    wanted = jnp.concatenate([wanted, south[2, :, -1:], north[2, :, :1]], axis=1)
    lat_index = lax.axis_index("lat")
    state = None
    slots = slot_of(owners, n_lat)
    each = max(1, min(num_steps, TABLE_BYTES // (n_lon * n_lat * step_rows * lanes * 4)))
    for first in range(0, num_steps, each):
        last = min(first + each, num_steps)
        local = jnp.arange(num_steps, dtype=jnp.int32)[:, None] - first
        row = (slots * (last - first) + local) * step_rows
        base = row + 2 * wanted
        grad = row + 2 * blocks + 4 * wanted
        state = run_steps(
            first,
            last,
            -0.5 / num_steps,
            step_rows,
            base,
            grad,
            edge_cells,
            seed_cells,
            items,
            state,
        )
    flow, edge, out, sides = state
    inner = swap(sides, "lon", (1,))
    outer = lax.ppermute(
        sides, "lon", [(i, (i + (1 if i % 2 else -1)) % n_lon) for i in range(n_lon)]
    )
    flags = jnp.stack([lax.axis_index("lon") % 2, lat_index == 0, lat_index == n_lat - 1])
    vmem = pl.BlockSpec(memory_space=pltpu.VMEM)
    field = pl.pallas_call(
        stretch_kernel,
        out_shape=jax.ShapeDtypeStruct((rows, lanes), jnp.float32),
        in_specs=[pl.BlockSpec(memory_space=pltpu.SMEM)] + [vmem] * 4,
        out_specs=vmem,
        compiler_params=pltpu.CompilerParams(vmem_limit_bytes=16 << 20),
        name="stretch",
    )(flags.astype(jnp.int32), flow, edge, inner, outer)
    return (out, field)


def solution(mesh):
    in_specs = (
        P("lon", "lat", None, None, None, None),
        P("lon", "lat", None, None, None, None),
        P("lon", "lat", None, None, None),
        P("lon", "lat", None, None),
        P(None, "lat", "lon"),
    )
    out_specs = (P(None, "lat", "lon"), P("lat", "lon"))
    return jax.shard_map(body, mesh=mesh, in_specs=in_specs, out_specs=out_specs, check_vma=False)
```

```python
import functools

import jax
import jax.numpy as jnp
from jax import lax
from jax.experimental import pallas as pl
from jax.experimental.pallas import tpu as pltpu
from jax.sharding import PartitionSpec as P

GROUP_ROWS = 4
TABLE_BYTES = 13 << 20
EARLY = ((0, 1, 2, 3, 4, 5),)
LATE = (6, 7)
WAITS = {
    "z3": ("z1",),
    "edge": ("z1",),
    "r1.1": ("z1",),
    "r2.1": ("z1",),
    "r1.2": ("r0.2",),
    "r2.2": ("z2",),
    "c1": ("r2.1",),
    "c2": ("r3.1",),
    "c3": ("r1.1",),
}


def after(value, *earlier):
    return lax.optimization_barrier((value, *earlier))[0] if earlier else value


def swap(value, axis, masks):
    count = lax.axis_size(axis)
    pairs = [(i, i ^ masks[i % len(masks)]) for i in range(count)]
    return lax.ppermute(value, axis, pairs)


def plane_masks(n_lon):
    bits = []
    mask = 2
    while mask < n_lon:
        bits.append(mask)
        mask *= 2
    return bits, bits[::-1]


def slot_of(owners, n_lat):
    lon, lat = lax.axis_index("lon"), lax.axis_index("lat")
    even, odd = plane_masks(lax.axis_size("lon"))
    places = 1 << len(even)
    owner_lon, owner_lat = owners // n_lat, owners % n_lat
    apart = owner_lat ^ lat
    foreign = (owner_lon ^ lon) & 1
    base = lon ^ foreign
    diff = owner_lon ^ base
    place = jnp.zeros_like(owners)
    for position, (even_mask, odd_mask) in enumerate(zip(even, odd)):
        mask = jnp.where((base & 1) == 0, even_mask, odd_mask)
        place = place + jnp.where((diff & mask) != 0, 1 << position, 0)
    return (apart * 2 + foreign) * places + place


def advance(along_x, along_y, coeffs):
    vel_x, vel_y, xx, xy, yx, yy = coeffs
    half_x = vel_x + xx * along_x + xy * along_y
    half_y = vel_y + yx * along_x + yy * along_y
    full_x = half_x + half_x
    full_y = half_y + half_y
    third_x = full_x + (xx * half_x + xy * half_y)
    third_y = full_y + (yx * half_x + yy * half_y)
    ratio = 2.0 / 3.0
    second_x = full_x + ratio * (xx * third_x + xy * third_y)
    second_y = full_y + ratio * (yx * third_x + yy * third_y)
    new_x = along_x + (full_x + (xx * second_x + xy * second_y))
    new_y = along_y + (full_y + (yx * second_x + yy * second_y))
    return new_x, new_y


def widen_pieces(table, slots, pieces, first, steps, step_rows, scale):
    for slot, piece in zip(slots, pieces):

        def widen(part, carry, slot=slot, piece=piece):
            place, step = part // steps, part % steps
            source = pl.multiple_of((first + step) * step_rows, step_rows)
            row = pl.multiple_of((slot * steps + part) * step_rows, step_rows)
            values = piece[place, pl.ds(source, step_rows), :].astype(jnp.float32) * scale
            table[pl.ds(row, step_rows), :] = values
            return carry

        lax.fori_loop(0, piece.shape[0] * steps, widen, 0, unroll=4)


def widen_kernel(slots, has_table, first, steps, step_rows, scale, *refs):
    pieces = refs[1:-1] if has_table else refs[:-1]
    widen_pieces(refs[-1], slots, pieces, first, steps, step_rows, scale)


def run_widen(table, height, items, first, last, step_rows, scale):
    pieces = [item[0] for item in items]
    slots = tuple(item[1] for item in items)
    lanes = pieces[0].shape[-1]
    vmem = pl.BlockSpec(memory_space=pltpu.VMEM)
    given = [table] if table is not None else []
    return pl.pallas_call(
        functools.partial(
            widen_kernel, slots, table is not None, first, last - first, step_rows, scale
        ),
        out_shape=jax.ShapeDtypeStruct((height, lanes), jnp.float32),
        in_specs=[vmem] * len(given + pieces),
        out_specs=vmem,
        input_output_aliases={0: 0} if given else {},
        cost_estimate=pl.CostEstimate(flops=0, bytes_accessed=8 << 20, transcendentals=0),
        compiler_params=pltpu.CompilerParams(vmem_limit_bytes=4 << 20),
        name=f"widen_{first}",
    )(*given, *pieces)


def steps_kernel(first, scale, step_rows, slots, has_table, has_start, last, unroll, *refs):
    count = len(slots)
    rows_ref, edge_ref, cells_hbm = refs[:3]
    given = refs[4:] if has_table else refs[3:]
    pieces = given[:count]
    start_ref, start_edge = given[count : count + 2] if has_start else (None, None)
    rest = given[count + 2 :] if has_start else given[count:]
    table, rest = (rest[0], rest[1:]) if has_table else (rest[-4], rest)
    flow_ref, out_edge = rest[:2]
    out_hbm, out_sides = rest[2:4] if last else (None, None)
    cells_ref, arrived, written = rest[-3:]
    steps, rows, lanes = cells_ref.shape
    fetch = pltpu.make_async_copy(cells_hbm.at[pl.ds(first, steps)], cells_ref, arrived)
    fetch.start()
    widen_pieces(table, slots, pieces, first, steps, step_rows, scale)
    fetch.wait()
    upper = lax.broadcasted_iota(jnp.int32, (8, lanes), 0) < GROUP_ROWS
    lane = lax.broadcasted_iota(jnp.int32, (8, lanes), 1)
    zero = jnp.zeros((8, lanes), jnp.float32)
    groups = rows // GROUP_ROWS

    def begin_at(ref, row):
        return (ref[0, pl.ds(row, 8), :], ref[1, pl.ds(row, 8), :]) if has_start else (zero, zero)

    def tile(one, two, indices, along_x, along_y):
        for step in range(steps):
            index = indices(step)
            sources = [
                (rows_ref[kind, first + step, one] + k, rows_ref[kind, first + step, two] + k)
                for kind, number in ((0, 2), (1, 4))
                for k in range(number)
            ]
            coeffs = []
            for above, below in sources:
                values = jnp.where(
                    upper,
                    jnp.broadcast_to(table[pl.ds(above, 1), :], (8, lanes)),
                    jnp.broadcast_to(table[pl.ds(below, 1), :], (8, lanes)),
                )
                coeffs.append(
                    jnp.take_along_axis(values, index, axis=1, mode="promise_in_bounds")
                )
            along_x, along_y = advance(along_x, along_y, coeffs)
        return along_x, along_y

    block = 8 * unroll

    def send(number):
        part = pl.ds(pl.multiple_of(number * block, block), block)
        return pltpu.make_async_copy(flow_ref.at[:, part], out_hbm.at[:, part], written.at[number])

    def tiles(number, carry):
        for inner in range(unroll):
            at = number * unroll + inner
            row = pl.multiple_of(at * 8, 8)
            start = begin_at(start_ref, row)
            end = tile(2 * at, 2 * at + 1, lambda step: cells_ref[step, pl.ds(row, 8), :], *start)
            flow_ref[0, pl.ds(row, 8), :], flow_ref[1, pl.ds(row, 8), :] = end
        if last:
            send(number).start()
        return carry

    lax.fori_loop(0, rows // block, tiles, 0)
    start = begin_at(start_edge, 0)
    end = tile(groups, groups + 1, lambda step: edge_ref[first + step], *start)
    out_edge[0], out_edge[1] = end
    if not last:
        return
    half = lanes // 2
    ends = jnp.where(lane < half, 0, lanes - 1)
    for part in range(2):
        sides = [zero] * 4
        for at in range(rows // 8):
            value = flow_ref[part, at * 8 : at * 8 + 8, :]
            value = jnp.take_along_axis(value, ends, axis=1, mode="promise_in_bounds")
            sides[at % 4] = jnp.where((lane & (half - 1)) == at, value, sides[at % 4])
        out_sides[part] = (sides[0] + sides[1]) + (sides[2] + sides[3])
    for number in range(rows // block):
        send(number).wait()


def run_steps(
    first, last, scale, step_rows, height, table_rows, edge_cells, cells, table, items, start
):
    num_steps, rows, lanes = cells.shape
    steps = last - first
    pieces = [item[0] for item in items]
    slots = tuple(item[1] for item in items)
    vmem = pl.BlockSpec(memory_space=pltpu.VMEM)
    smem = pl.BlockSpec(memory_space=pltpu.SMEM)
    hbm = pl.BlockSpec(memory_space=pltpu.HBM)
    need = steps * rows * lanes * 4
    small = jax.ShapeDtypeStruct((2, 8, lanes), jnp.float32)
    whole = jax.ShapeDtypeStruct((2, rows, lanes), jnp.float32)
    final = last == num_steps
    starts = list(start) if first else []
    given = [table] if table is not None else []
    shape = jax.ShapeDtypeStruct((height, lanes), jnp.float32)
    need += 0 if given else height * lanes * 4
    unroll = 8
    results = pl.pallas_call(
        functools.partial(
            steps_kernel, first, scale, step_rows, slots, len(given) > 0, first > 0, final, unroll
        ),
        out_shape=(shape,) * len(given) + (whole, small) + ((whole, small) if final else ()),
        in_specs=[smem, vmem, hbm] + [vmem] * len(given + pieces + starts),
        out_specs=(vmem,) * len(given) + (vmem, vmem) + ((hbm, vmem) if final else ()),
        input_output_aliases={3: 0} if given else {},
        scratch_shapes=([] if given else [pltpu.VMEM(shape.shape, shape.dtype)])
        + [
            pltpu.VMEM((steps, rows, lanes), jnp.int32),
            pltpu.SemaphoreType.DMA(()),
            pltpu.SemaphoreType.DMA((rows // 8 // unroll,)),
        ],
        cost_estimate=pl.CostEstimate(
            flops=40 * steps * rows * lanes, bytes_accessed=16 << 20, transcendentals=0
        ),
        compiler_params=pltpu.CompilerParams(vmem_limit_bytes=need + (4 << 20)),
        name=f"rk_steps_{first}",
    )(table_rows, edge_cells, cells, *given, *pieces, *starts)
    return results[len(given) :]


def stretch_kernel(flow_ref, edge_ref, sides_ref, out_ref):
    _, rows, lanes = flow_ref.shape
    half = lanes // 2
    lane = lax.broadcasted_iota(jnp.int32, (8, lanes), 1)
    row = lax.broadcasted_iota(jnp.int32, (8, lanes), 0)
    sides = [sides_ref[part] for part in range(2)]
    south = [edge_ref[part, 0:1, :] for part in range(2)]
    north = [edge_ref[part, GROUP_ROWS : GROUP_ROWS + 1, :] for part in range(2)]
    tiles = rows // 8
    for at in range(tiles):
        start = at * 8
        index = jnp.where(lane < half, half + at, at)
        diff_lon, diff_lat = [], []
        for part in range(2):
            flow = flow_ref[part, start : start + 8, :]
            halo = jnp.take_along_axis(sides[part], index, axis=1, mode="promise_in_bounds")
            left = jnp.where(lane == 0, halo, pltpu.roll(flow, 1, 1))
            right = jnp.where(lane == lanes - 1, halo, pltpu.roll(flow, lanes - 1, 1))
            diff_lon.append((right - left) * 0.5)
            under = south[part] if at == 0 else flow_ref[part, start - 1 : start, :]
            over = north[part] if at == tiles - 1 else flow_ref[part, start + 8 : start + 9, :]
            below = jnp.where(row == 0, jnp.broadcast_to(under, flow.shape), pltpu.roll(flow, 1, 0))
            above = jnp.where(row == 7, jnp.broadcast_to(over, flow.shape), pltpu.roll(flow, 7, 0))
            diff_lat.append((above - below) * 0.5)
        out_ref[start : start + 8, :] = stretch_rate(diff_lon, diff_lat)


def stretch_rate(diff_lon, diff_lat):
    map_xx = 1.0 + diff_lon[0]
    map_xy = diff_lat[0]
    map_yx = diff_lon[1]
    map_yy = 1.0 + diff_lat[1]
    green_xx = map_xx * map_xx + map_yx * map_yx
    green_yy = map_xy * map_xy + map_yy * map_yy
    green_xy = map_xx * map_xy + map_yx * map_yy
    half_diff = 0.5 * (green_xx - green_yy)
    largest = 0.5 * (green_xx + green_yy) + jnp.sqrt(half_diff * half_diff + green_xy * green_xy)
    return 0.5 * jnp.log(largest)


def body(vel_base, vel_grad, route_dev, route_block, seed_cells):
    n_lon, n_lat = lax.axis_size("lon"), lax.axis_size("lat")
    num_steps, rows, lanes = seed_cells.shape
    blocks = vel_base.shape[3]
    step_rows = 6 * blocks
    shard = jnp.concatenate(
        [
            vel_base.reshape(num_steps, 2 * blocks, lanes),
            vel_grad.reshape(num_steps, 4 * blocks, lanes),
        ],
        axis=1,
    ).reshape(num_steps * step_rows, lanes)
    places = n_lon // 2
    owners = route_dev[0, 0, :, :, 0]
    wanted = route_block[0, 0]
    done = {}

    def gated(value, label):
        return after(value, *[done[name] for name in WAITS.get(label, ())])

    came = [shard]
    for apart in range(1, n_lat):
        done[f"z{apart}"] = swap(gated(shard, f"z{apart}"), "lat", (apart,))
        came.append(done[f"z{apart}"])
    even, odd = plane_masks(n_lon)
    held = [value[None] for value in came]
    for stage, masks in enumerate(zip(even, odd)):
        for apart in range(n_lat):
            label = f"r{apart}.{stage + 1}"
            sent = gated(held[apart], label)
            done[label] = swap(sent, "lon", masks)
            held[apart] = jnp.concatenate([sent, done[label]])
    def edge_of(row):
        value = jnp.stack([seed_cells[:, row, :], owners, wanted])
        return gated(value, "edge")

    south = lax.ppermute(edge_of(-1), "lat", [(i, i + 1) for i in range(n_lat - 1)])
    north = lax.ppermute(edge_of(0), "lat", [(i + 1, i) for i in range(n_lat - 1)])
    edge_cells = jnp.repeat(jnp.stack([south[0], north[0]], axis=1), GROUP_ROWS, axis=1)
    owners = jnp.concatenate([owners, south[1, :, -1:], north[1, :, :1]], axis=1)
    wanted = jnp.concatenate([wanted, south[2, :, -1:], north[2, :, :1]], axis=1)
    lat_index = lax.axis_index("lat")
    each = max(1, min(num_steps, TABLE_BYTES // (n_lon * n_lat * step_rows * lanes * 4)))
    spans = [(first, min(first + each, num_steps)) for first in range(0, num_steps, each)]
    slots = slot_of(owners, n_lat)
    local = jnp.arange(num_steps, dtype=jnp.int32)[:, None]
    rows_of = []
    for first, last in spans:
        row = (slots * (last - first) + local - first) * step_rows
        rows_of.append(jnp.stack([row + 2 * wanted, row + 2 * blocks + 4 * wanted]))
    done["rows"] = rows_of[-1]
    items = []
    for apart in range(n_lat):
        other = swap(gated(held[apart], f"c{apart}"), "lon", (1,))
        items += [(held[apart], 2 * apart * places), (other, (2 * apart + 1) * places)]
    state = None
    for (first, last), table_rows in zip(spans, rows_of):
        height = len(items) * places * (last - first) * step_rows
        scale = -0.5 / num_steps
        table = None
        for chosen in EARLY:
            chosen = [items[number] for number in chosen]
            table = run_widen(table, height, chosen, first, last, step_rows, scale)
        chosen = [items[number] for number in LATE]
        state = run_steps(
            first,
            last,
            scale,
            step_rows,
            height,
            table_rows,
            edge_cells,
            seed_cells,
            table,
            chosen,
            state,
        )
    flow, edge, out, sides = state
    inner = swap(sides, "lon", (1,))
    outer = lax.ppermute(
        sides, "lon", [(i, (i + (1 if i % 2 else -1)) % n_lon) for i in range(n_lon)]
    )
    south = jnp.where(lat_index == 0, flow[:, :1], edge[:, :1])
    north = jnp.where(lat_index == n_lat - 1, flow[:, -1:], edge[:, GROUP_ROWS : GROUP_ROWS + 1])
    edge = jnp.repeat(jnp.concatenate([south, north], axis=1), GROUP_ROWS, axis=1)
    lane = lax.broadcasted_iota(jnp.int32, sides.shape, 2)
    from_inner = (lane < lanes // 2) == (lax.axis_index("lon") % 2 == 0)
    sides = jnp.where(from_inner, inner, outer)
    vmem = pl.BlockSpec(memory_space=pltpu.VMEM)
    field = pl.pallas_call(
        stretch_kernel,
        out_shape=jax.ShapeDtypeStruct((rows, lanes), jnp.float32),
        in_specs=[vmem] * 3,
        out_specs=vmem,
        compiler_params=pltpu.CompilerParams(vmem_limit_bytes=16 << 20),
        name="stretch",
    )(flow, edge, sides)
    return (out, field)


def solution(mesh):
    in_specs = (
        P("lon", "lat", None, None, None, None),
        P("lon", "lat", None, None, None, None),
        P("lon", "lat", None, None, None),
        P("lon", "lat", None, None),
        P(None, "lat", "lon"),
    )
    out_specs = (P(None, "lat", "lon"), P("lat", "lon"))
    return jax.shard_map(body, mesh=mesh, in_specs=in_specs, out_specs=out_specs, check_vma=False)
```

```python
import functools

import jax
import jax.numpy as jnp
from jax import lax
from jax.experimental import pallas as pl
from jax.experimental.pallas import tpu as pltpu
from jax.sharding import PartitionSpec as P

GROUP_ROWS = 4
TABLE_BYTES = 13 << 20
EARLY = ((0, 1, 2, 3, 4, 5),)
LATE = (6, 7)
WAITS = {
    "z3": ("z1",),
    "edge": ("z1",),
    "r1.1": ("z1",),
    "r2.1": ("z1",),
    "r1.2": ("r0.2",),
    "r2.2": ("z2",),
    "c1": ("r2.1",),
    "c2": ("r3.1",),
}


def after(value, *earlier):
    return lax.optimization_barrier((value, *earlier))[0] if earlier else value


def swap(value, axis, masks):
    count = lax.axis_size(axis)
    pairs = [(i, i ^ masks[i % len(masks)]) for i in range(count)]
    return lax.ppermute(value, axis, pairs)


def plane_masks(n_lon):
    bits = []
    mask = 2
    while mask < n_lon:
        bits.append(mask)
        mask *= 2
    return bits, bits[::-1]


def slot_of(owners, n_lat):
    lon, lat = lax.axis_index("lon"), lax.axis_index("lat")
    even, odd = plane_masks(lax.axis_size("lon"))
    places = 1 << len(even)
    owner_lon, owner_lat = owners // n_lat, owners % n_lat
    apart = owner_lat ^ lat
    foreign = (owner_lon ^ lon) & 1
    base = lon ^ foreign
    diff = owner_lon ^ base
    place = jnp.zeros_like(owners)
    for position, (even_mask, odd_mask) in enumerate(zip(even, odd)):
        mask = jnp.where((base & 1) == 0, even_mask, odd_mask)
        place = place + jnp.where((diff & mask) != 0, 1 << position, 0)
    return (apart * 2 + foreign) * places + place


def advance(along_x, along_y, coeffs):
    vel_x, vel_y, xx, xy, yx, yy = coeffs
    half_x = vel_x + xx * along_x + xy * along_y
    half_y = vel_y + yx * along_x + yy * along_y
    full_x = half_x + half_x
    full_y = half_y + half_y
    third_x = full_x + (xx * half_x + xy * half_y)
    third_y = full_y + (yx * half_x + yy * half_y)
    ratio = 2.0 / 3.0
    second_x = full_x + ratio * (xx * third_x + xy * third_y)
    second_y = full_y + ratio * (yx * third_x + yy * third_y)
    new_x = along_x + (full_x + (xx * second_x + xy * second_y))
    new_y = along_y + (full_y + (yx * second_x + yy * second_y))
    return new_x, new_y


def widen_pieces(table, slots, pieces, first, steps, step_rows, scale):
    for slot, piece in zip(slots, pieces):

        def widen(part, carry, slot=slot, piece=piece):
            place, step = part // steps, part % steps
            source = pl.multiple_of((first + step) * step_rows, step_rows)
            row = pl.multiple_of((slot * steps + part) * step_rows, step_rows)
            values = piece[place, pl.ds(source, step_rows), :].astype(jnp.float32) * scale
            table[pl.ds(row, step_rows), :] = values
            return carry

        lax.fori_loop(0, piece.shape[0] * steps, widen, 0, unroll=4)


def widen_kernel(slots, has_table, first, steps, step_rows, scale, *refs):
    pieces = refs[1:-1] if has_table else refs[:-1]
    widen_pieces(refs[-1], slots, pieces, first, steps, step_rows, scale)


def run_widen(table, height, items, first, last, step_rows, scale):
    pieces = [item[0] for item in items]
    slots = tuple(item[1] for item in items)
    lanes = pieces[0].shape[-1]
    vmem = pl.BlockSpec(memory_space=pltpu.VMEM)
    given = [table] if table is not None else []
    return pl.pallas_call(
        functools.partial(
            widen_kernel, slots, table is not None, first, last - first, step_rows, scale
        ),
        out_shape=jax.ShapeDtypeStruct((height, lanes), jnp.float32),
        in_specs=[vmem] * len(given + pieces),
        out_specs=vmem,
        input_output_aliases={0: 0} if given else {},
        cost_estimate=pl.CostEstimate(flops=0, bytes_accessed=8 << 20, transcendentals=0),
        compiler_params=pltpu.CompilerParams(vmem_limit_bytes=4 << 20),
        name=f"widen_{first}",
    )(*given, *pieces)


def steps_kernel(first, scale, step_rows, slots, has_table, has_start, last, unroll, *refs):
    count = len(slots)
    rows_ref, edge_ref, cells_hbm = refs[:3]
    given = refs[4:] if has_table else refs[3:]
    pieces = given[:count]
    start_ref, start_edge = given[count : count + 2] if has_start else (None, None)
    rest = given[count + 2 :] if has_start else given[count:]
    table, rest = (rest[0], rest[1:]) if has_table else (rest[-4], rest)
    flow_ref, out_edge = rest[:2]
    out_hbm, out_sides = rest[2:4] if last else (None, None)
    cells_ref, arrived, written = rest[-3:]
    steps, rows, lanes = cells_ref.shape
    fetch = pltpu.make_async_copy(cells_hbm.at[pl.ds(first, steps)], cells_ref, arrived)
    fetch.start()
    widen_pieces(table, slots, pieces, first, steps, step_rows, scale)
    fetch.wait()
    upper = lax.broadcasted_iota(jnp.int32, (8, lanes), 0) < GROUP_ROWS
    lane = lax.broadcasted_iota(jnp.int32, (8, lanes), 1)
    zero = jnp.zeros((8, lanes), jnp.float32)
    groups = rows // GROUP_ROWS
    blocks = step_rows // 6
    shift = (blocks - 1).bit_length()

    def begin_at(ref, row):
        return (ref[0, pl.ds(row, 8), :], ref[1, pl.ds(row, 8), :]) if has_start else (zero, zero)

    def tile(one, two, indices, along_x, along_y):
        for step in range(steps):
            index = indices(step)
            places = []
            for which in (one, two):
                code = rows_ref[first + step, which]
                block = code & ((1 << shift) - 1)
                start = lax.shift_right_logical(code, shift)
                places.append((start + 2 * block, start + 2 * blocks + 4 * block))
            sources = [
                (places[0][kind] + k, places[1][kind] + k)
                for kind, number in ((0, 2), (1, 4))
                for k in range(number)
            ]
            coeffs = []
            for above, below in sources:
                values = jnp.where(
                    upper,
                    jnp.broadcast_to(table[pl.ds(above, 1), :], (8, lanes)),
                    jnp.broadcast_to(table[pl.ds(below, 1), :], (8, lanes)),
                )
                coeffs.append(
                    jnp.take_along_axis(values, index, axis=1, mode="promise_in_bounds")
                )
            along_x, along_y = advance(along_x, along_y, coeffs)
        return along_x, along_y

    block = 8 * unroll

    def send(number):
        part = pl.ds(pl.multiple_of(number * block, block), block)
        return pltpu.make_async_copy(flow_ref.at[:, part], out_hbm.at[:, part], written.at[number])

    def tiles(number, carry):
        for inner in range(unroll):
            at = number * unroll + inner
            row = pl.multiple_of(at * 8, 8)
            start = begin_at(start_ref, row)
            end = tile(2 * at, 2 * at + 1, lambda step: cells_ref[step, pl.ds(row, 8), :], *start)
            flow_ref[0, pl.ds(row, 8), :], flow_ref[1, pl.ds(row, 8), :] = end
        if last:
            send(number).start()
        return carry

    lax.fori_loop(0, rows // block, tiles, 0)
    start = begin_at(start_edge, 0)
    end = tile(groups, groups + 1, lambda step: edge_ref[first + step], *start)
    out_edge[0], out_edge[1] = end
    if not last:
        return
    half = lanes // 2
    ends = jnp.where(lane < half, 0, lanes - 1)
    for part in range(2):
        sides = [zero] * 4
        for at in range(rows // 8):
            value = flow_ref[part, at * 8 : at * 8 + 8, :]
            value = jnp.take_along_axis(value, ends, axis=1, mode="promise_in_bounds")
            sides[at % 4] = jnp.where((lane & (half - 1)) == at, value, sides[at % 4])
        out_sides[part] = (sides[0] + sides[1]) + (sides[2] + sides[3])
    for number in range(rows // block):
        send(number).wait()


def run_steps(
    first, last, scale, step_rows, height, table_rows, edge_cells, cells, table, items, start
):
    num_steps, rows, lanes = cells.shape
    steps = last - first
    pieces = [item[0] for item in items]
    slots = tuple(item[1] for item in items)
    vmem = pl.BlockSpec(memory_space=pltpu.VMEM)
    smem = pl.BlockSpec(memory_space=pltpu.SMEM)
    hbm = pl.BlockSpec(memory_space=pltpu.HBM)
    need = steps * rows * lanes * 4
    small = jax.ShapeDtypeStruct((2, 8, lanes), jnp.float32)
    whole = jax.ShapeDtypeStruct((2, rows, lanes), jnp.float32)
    final = last == num_steps
    starts = list(start) if first else []
    given = [table] if table is not None else []
    shape = jax.ShapeDtypeStruct((height, lanes), jnp.float32)
    need += 0 if given else height * lanes * 4
    unroll = 8
    results = pl.pallas_call(
        functools.partial(
            steps_kernel, first, scale, step_rows, slots, len(given) > 0, first > 0, final, unroll
        ),
        out_shape=(shape,) * len(given) + (whole, small) + ((whole, small) if final else ()),
        in_specs=[smem, vmem, hbm] + [vmem] * len(given + pieces + starts),
        out_specs=(vmem,) * len(given) + (vmem, vmem) + ((hbm, vmem) if final else ()),
        input_output_aliases={3: 0} if given else {},
        scratch_shapes=([] if given else [pltpu.VMEM(shape.shape, shape.dtype)])
        + [
            pltpu.VMEM((steps, rows, lanes), jnp.int32),
            pltpu.SemaphoreType.DMA(()),
            pltpu.SemaphoreType.DMA((rows // 8 // unroll,)),
        ],
        cost_estimate=pl.CostEstimate(
            flops=40 * steps * rows * lanes, bytes_accessed=16 << 20, transcendentals=0
        ),
        compiler_params=pltpu.CompilerParams(vmem_limit_bytes=need + (4 << 20)),
        name=f"rk_steps_{first}",
    )(table_rows, edge_cells, cells, *given, *pieces, *starts)
    return results[len(given) :]


def stretch_kernel(flow_ref, edge_ref, sides_ref, out_ref):
    _, rows, lanes = flow_ref.shape
    half = lanes // 2
    lane = lax.broadcasted_iota(jnp.int32, (8, lanes), 1)
    row = lax.broadcasted_iota(jnp.int32, (8, lanes), 0)
    sides = [sides_ref[part] for part in range(2)]
    south = [edge_ref[part, 0:1, :] for part in range(2)]
    north = [edge_ref[part, GROUP_ROWS : GROUP_ROWS + 1, :] for part in range(2)]
    tiles = rows // 8
    for at in range(tiles):
        start = at * 8
        index = jnp.where(lane < half, half + at, at)
        diff_lon, diff_lat = [], []
        for part in range(2):
            flow = flow_ref[part, start : start + 8, :]
            halo = jnp.take_along_axis(sides[part], index, axis=1, mode="promise_in_bounds")
            left = jnp.where(lane == 0, halo, pltpu.roll(flow, 1, 1))
            right = jnp.where(lane == lanes - 1, halo, pltpu.roll(flow, lanes - 1, 1))
            diff_lon.append((right - left) * 0.5)
            under = south[part] if at == 0 else flow_ref[part, start - 1 : start, :]
            over = north[part] if at == tiles - 1 else flow_ref[part, start + 8 : start + 9, :]
            below = jnp.where(row == 0, jnp.broadcast_to(under, flow.shape), pltpu.roll(flow, 1, 0))
            above = jnp.where(row == 7, jnp.broadcast_to(over, flow.shape), pltpu.roll(flow, 7, 0))
            diff_lat.append((above - below) * 0.5)
        out_ref[start : start + 8, :] = stretch_rate(diff_lon, diff_lat)


def stretch_rate(diff_lon, diff_lat):
    map_xx = 1.0 + diff_lon[0]
    map_xy = diff_lat[0]
    map_yx = diff_lon[1]
    map_yy = 1.0 + diff_lat[1]
    green_xx = map_xx * map_xx + map_yx * map_yx
    green_yy = map_xy * map_xy + map_yy * map_yy
    green_xy = map_xx * map_xy + map_yx * map_yy
    half_diff = 0.5 * (green_xx - green_yy)
    largest = 0.5 * (green_xx + green_yy) + jnp.sqrt(half_diff * half_diff + green_xy * green_xy)
    return 0.5 * jnp.log(largest)


def body(vel_base, vel_grad, route_dev, route_block, seed_cells):
    n_lon, n_lat = lax.axis_size("lon"), lax.axis_size("lat")
    num_steps, rows, lanes = seed_cells.shape
    blocks = vel_base.shape[3]
    step_rows = 6 * blocks
    shard = jnp.concatenate(
        [
            vel_base.reshape(num_steps, 2 * blocks, lanes),
            vel_grad.reshape(num_steps, 4 * blocks, lanes),
        ],
        axis=1,
    ).reshape(num_steps * step_rows, lanes)
    places = n_lon // 2
    owners = route_dev[0, 0, :, :, 0]
    wanted = route_block[0, 0]
    done = {}

    def gated(value, label):
        return after(value, *[done[name] for name in WAITS.get(label, ())])

    came = [shard]
    for apart in range(1, n_lat):
        done[f"z{apart}"] = swap(gated(shard, f"z{apart}"), "lat", (apart,))
        came.append(done[f"z{apart}"])
    even, odd = plane_masks(n_lon)
    held = [value[None] for value in came]
    for stage, masks in enumerate(zip(even, odd)):
        for apart in range(n_lat):
            label = f"r{apart}.{stage + 1}"
            sent = gated(held[apart], label)
            done[label] = swap(sent, "lon", masks)
            held[apart] = jnp.concatenate([sent, done[label]])
    def edge_of(row):
        value = jnp.stack([seed_cells[:, row, :], owners, wanted])
        return gated(value, "edge")

    south = lax.ppermute(edge_of(-1), "lat", [(i, i + 1) for i in range(n_lat - 1)])
    north = lax.ppermute(edge_of(0), "lat", [(i + 1, i) for i in range(n_lat - 1)])
    edge_cells = jnp.repeat(jnp.stack([south[0], north[0]], axis=1), GROUP_ROWS, axis=1)
    owners = jnp.concatenate([owners, south[1, :, -1:], north[1, :, :1]], axis=1)
    wanted = jnp.concatenate([wanted, south[2, :, -1:], north[2, :, :1]], axis=1)
    lat_index = lax.axis_index("lat")
    each = max(1, min(num_steps, TABLE_BYTES // (n_lon * n_lat * step_rows * lanes * 4)))
    spans = [(first, min(first + each, num_steps)) for first in range(0, num_steps, each)]
    slots = slot_of(owners, n_lat)
    local = jnp.arange(num_steps, dtype=jnp.int32)[:, None]
    rows_of = []
    for first, last in spans:
        row = (slots * (last - first) + local - first) * step_rows
        rows_of.append((row << (blocks - 1).bit_length()) + wanted)
    items = []
    for apart in range(n_lat):
        other = swap(gated(held[apart], f"c{apart}"), "lon", (1,))
        items += [(held[apart], 2 * apart * places), (other, (2 * apart + 1) * places)]
    state = None
    for (first, last), table_rows in zip(spans, rows_of):
        height = len(items) * places * (last - first) * step_rows
        scale = -0.5 / num_steps
        table = None
        for chosen in EARLY:
            chosen = [items[number] for number in chosen]
            table = run_widen(table, height, chosen, first, last, step_rows, scale)
        chosen = [items[number] for number in LATE]
        state = run_steps(
            first,
            last,
            scale,
            step_rows,
            height,
            table_rows,
            edge_cells,
            seed_cells,
            table,
            chosen,
            state,
        )
    flow, edge, out, sides = state
    inner = swap(sides, "lon", (1,))
    outer = lax.ppermute(
        sides, "lon", [(i, (i + (1 if i % 2 else -1)) % n_lon) for i in range(n_lon)]
    )
    south = jnp.where(lat_index == 0, flow[:, :1], edge[:, :1])
    north = jnp.where(lat_index == n_lat - 1, flow[:, -1:], edge[:, GROUP_ROWS : GROUP_ROWS + 1])
    edge = jnp.repeat(jnp.concatenate([south, north], axis=1), GROUP_ROWS, axis=1)
    lane = lax.broadcasted_iota(jnp.int32, sides.shape, 2)
    from_inner = (lane < lanes // 2) == (lax.axis_index("lon") % 2 == 0)
    sides = jnp.where(from_inner, inner, outer)
    vmem = pl.BlockSpec(memory_space=pltpu.VMEM)
    field = pl.pallas_call(
        stretch_kernel,
        out_shape=jax.ShapeDtypeStruct((rows, lanes), jnp.float32),
        in_specs=[vmem] * 3,
        out_specs=vmem,
        compiler_params=pltpu.CompilerParams(vmem_limit_bytes=16 << 20),
        name="stretch",
    )(flow, edge, sides)
    return (out, field)


def solution(mesh):
    in_specs = (
        P("lon", "lat", None, None, None, None),
        P("lon", "lat", None, None, None, None),
        P("lon", "lat", None, None, None),
        P("lon", "lat", None, None),
        P(None, "lat", "lon"),
    )
    out_specs = (P(None, "lat", "lon"), P("lat", "lon"))
    return jax.shard_map(body, mesh=mesh, in_specs=in_specs, out_specs=out_specs, check_vma=False)
```

```python
import functools

import jax
import jax.numpy as jnp
from jax import lax
from jax.experimental import pallas as pl
from jax.experimental.pallas import tpu as pltpu
from jax.sharding import PartitionSpec as P

GROUP_ROWS = 4
TABLE_BYTES = 13 << 20
EARLY = ((0, 1, 2, 3, 4, 5),)
LATE = (6, 7)
WAITS = {
    "z3": ("z1",),
    "edge": ("z1",),
    "r1.1": ("z1",),
    "r2.1": ("z1",),
    "r1.2": ("r0.2",),
    "r2.2": ("z2",),
    "c1": ("r2.1",),
    "c2": ("r3.1",),
}


def after(value, *earlier):
    return lax.optimization_barrier((value, *earlier))[0] if earlier else value


def swap(value, axis, masks):
    count = lax.axis_size(axis)
    pairs = [(i, i ^ masks[i % len(masks)]) for i in range(count)]
    return lax.ppermute(value, axis, pairs)


def plane_masks(n_lon):
    bits = []
    mask = 2
    while mask < n_lon:
        bits.append(mask)
        mask *= 2
    return bits, bits[::-1]


def slot_of(owners, n_lat):
    lon, lat = lax.axis_index("lon"), lax.axis_index("lat")
    even, odd = plane_masks(lax.axis_size("lon"))
    places = 1 << len(even)
    owner_lon, owner_lat = owners // n_lat, owners % n_lat
    apart = owner_lat ^ lat
    foreign = (owner_lon ^ lon) & 1
    base = lon ^ foreign
    diff = owner_lon ^ base
    place = jnp.zeros_like(owners)
    for position, (even_mask, odd_mask) in enumerate(zip(even, odd)):
        mask = jnp.where((base & 1) == 0, even_mask, odd_mask)
        place = place + jnp.where((diff & mask) != 0, 1 << position, 0)
    return (apart * 2 + foreign) * places + place


def advance(along_x, along_y, coeffs):
    vel_x, vel_y, xx, xy, yx, yy = coeffs
    half_x = vel_x + xx * along_x + xy * along_y
    half_y = vel_y + yx * along_x + yy * along_y
    full_x = half_x + half_x
    full_y = half_y + half_y
    third_x = full_x + (xx * half_x + xy * half_y)
    third_y = full_y + (yx * half_x + yy * half_y)
    ratio = 2.0 / 3.0
    second_x = full_x + ratio * (xx * third_x + xy * third_y)
    second_y = full_y + ratio * (yx * third_x + yy * third_y)
    new_x = along_x + (full_x + (xx * second_x + xy * second_y))
    new_y = along_y + (full_y + (yx * second_x + yy * second_y))
    return new_x, new_y


def widen_pieces(table, slots, pieces, first, steps, step_rows, scale):
    for slot, piece in zip(slots, pieces):

        def widen(part, carry, slot=slot, piece=piece):
            place, step = part // steps, part % steps
            source = pl.multiple_of((first + step) * step_rows, step_rows)
            row = pl.multiple_of((slot * steps + part) * step_rows, step_rows)
            values = piece[place, pl.ds(source, step_rows), :].astype(jnp.float32) * scale
            table[pl.ds(row, step_rows), :] = values
            return carry

        lax.fori_loop(0, piece.shape[0] * steps, widen, 0, unroll=8)


def widen_kernel(slots, has_table, first, steps, step_rows, scale, *refs):
    pieces = refs[1:-1] if has_table else refs[:-1]
    widen_pieces(refs[-1], slots, pieces, first, steps, step_rows, scale)


def run_widen(table, height, items, first, last, step_rows, scale):
    pieces = [item[0] for item in items]
    slots = tuple(item[1] for item in items)
    lanes = pieces[0].shape[-1]
    vmem = pl.BlockSpec(memory_space=pltpu.VMEM)
    given = [table] if table is not None else []
    return pl.pallas_call(
        functools.partial(
            widen_kernel, slots, table is not None, first, last - first, step_rows, scale
        ),
        out_shape=jax.ShapeDtypeStruct((height, lanes), jnp.float32),
        in_specs=[vmem] * len(given + pieces),
        out_specs=vmem,
        input_output_aliases={0: 0} if given else {},
        cost_estimate=pl.CostEstimate(flops=0, bytes_accessed=8 << 20, transcendentals=0),
        compiler_params=pltpu.CompilerParams(vmem_limit_bytes=4 << 20),
        name=f"widen_{first}",
    )(*given, *pieces)


def steps_kernel(first, scale, step_rows, slots, has_table, has_start, last, unroll, *refs):
    count = len(slots)
    rows_ref, edge_ref, cells_hbm = refs[:3]
    given = refs[4:] if has_table else refs[3:]
    pieces = given[:count]
    start_ref, start_edge = given[count : count + 2] if has_start else (None, None)
    rest = given[count + 2 :] if has_start else given[count:]
    table, rest = (rest[0], rest[1:]) if has_table else (rest[-4], rest)
    flow_ref, out_edge = rest[:2]
    out_hbm, out_sides = rest[2:4] if last else (None, None)
    cells_ref, arrived, written = rest[-3:]
    steps, rows, lanes = cells_ref.shape
    fetch = pltpu.make_async_copy(cells_hbm.at[pl.ds(first, steps)], cells_ref, arrived)
    fetch.start()
    widen_pieces(table, slots, pieces, first, steps, step_rows, scale)
    fetch.wait()
    upper = lax.broadcasted_iota(jnp.int32, (8, lanes), 0) < GROUP_ROWS
    lane = lax.broadcasted_iota(jnp.int32, (8, lanes), 1)
    zero = jnp.zeros((8, lanes), jnp.float32)
    groups = rows // GROUP_ROWS
    blocks = step_rows // 6
    shift = (blocks - 1).bit_length()

    def begin_at(ref, row):
        return (ref[0, pl.ds(row, 8), :], ref[1, pl.ds(row, 8), :]) if has_start else (zero, zero)

    def tile(one, two, indices, along_x, along_y):
        for step in range(steps):
            index = indices(step)
            places = []
            for which in (one, two):
                code = rows_ref[first + step, which]
                block = code & ((1 << shift) - 1)
                start = lax.shift_right_logical(code, shift)
                places.append((start + 2 * block, start + 2 * blocks + 4 * block))
            sources = [
                (places[0][kind] + k, places[1][kind] + k)
                for kind, number in ((0, 2), (1, 4))
                for k in range(number)
            ]
            coeffs = []
            for above, below in sources:
                values = jnp.where(
                    upper,
                    jnp.broadcast_to(table[pl.ds(above, 1), :], (8, lanes)),
                    jnp.broadcast_to(table[pl.ds(below, 1), :], (8, lanes)),
                )
                coeffs.append(
                    jnp.take_along_axis(values, index, axis=1, mode="promise_in_bounds")
                )
            along_x, along_y = advance(along_x, along_y, coeffs)
        return along_x, along_y

    block = 8 * unroll

    def send(number):
        part = pl.ds(pl.multiple_of(number * block, block), block)
        return pltpu.make_async_copy(flow_ref.at[:, part], out_hbm.at[:, part], written.at[number])

    def tiles(number, carry):
        for inner in range(unroll):
            at = number * unroll + inner
            row = pl.multiple_of(at * 8, 8)
            start = begin_at(start_ref, row)
            end = tile(2 * at, 2 * at + 1, lambda step: cells_ref[step, pl.ds(row, 8), :], *start)
            flow_ref[0, pl.ds(row, 8), :], flow_ref[1, pl.ds(row, 8), :] = end
        if last:
            send(number).start()
        return carry

    lax.fori_loop(0, rows // block, tiles, 0)
    start = begin_at(start_edge, 0)
    end = tile(groups, groups + 1, lambda step: edge_ref[first + step], *start)
    out_edge[0], out_edge[1] = end
    if not last:
        return
    half = lanes // 2
    ends = jnp.where(lane < half, 0, lanes - 1)
    for part in range(2):
        sides = [zero] * 4
        for at in range(rows // 8):
            value = flow_ref[part, at * 8 : at * 8 + 8, :]
            value = jnp.take_along_axis(value, ends, axis=1, mode="promise_in_bounds")
            sides[at % 4] = jnp.where((lane & (half - 1)) == at, value, sides[at % 4])
        out_sides[part] = (sides[0] + sides[1]) + (sides[2] + sides[3])
    for number in range(rows // block):
        send(number).wait()


def run_steps(
    first, last, scale, step_rows, height, table_rows, edge_cells, cells, table, items, start
):
    num_steps, rows, lanes = cells.shape
    steps = last - first
    pieces = [item[0] for item in items]
    slots = tuple(item[1] for item in items)
    vmem = pl.BlockSpec(memory_space=pltpu.VMEM)
    smem = pl.BlockSpec(memory_space=pltpu.SMEM)
    hbm = pl.BlockSpec(memory_space=pltpu.HBM)
    need = steps * rows * lanes * 4
    small = jax.ShapeDtypeStruct((2, 8, lanes), jnp.float32)
    whole = jax.ShapeDtypeStruct((2, rows, lanes), jnp.float32)
    final = last == num_steps
    starts = list(start) if first else []
    given = [table] if table is not None else []
    shape = jax.ShapeDtypeStruct((height, lanes), jnp.float32)
    need += 0 if given else height * lanes * 4
    unroll = 16
    results = pl.pallas_call(
        functools.partial(
            steps_kernel, first, scale, step_rows, slots, len(given) > 0, first > 0, final, unroll
        ),
        out_shape=(shape,) * len(given) + (whole, small) + ((whole, small) if final else ()),
        in_specs=[smem, vmem, hbm] + [vmem] * len(given + pieces + starts),
        out_specs=(vmem,) * len(given) + (vmem, vmem) + ((hbm, vmem) if final else ()),
        input_output_aliases={3: 0} if given else {},
        scratch_shapes=([] if given else [pltpu.VMEM(shape.shape, shape.dtype)])
        + [
            pltpu.VMEM((steps, rows, lanes), jnp.int32),
            pltpu.SemaphoreType.DMA(()),
            pltpu.SemaphoreType.DMA((rows // 8 // unroll,)),
        ],
        cost_estimate=pl.CostEstimate(
            flops=40 * steps * rows * lanes, bytes_accessed=16 << 20, transcendentals=0
        ),
        compiler_params=pltpu.CompilerParams(vmem_limit_bytes=need + (4 << 20)),
        name=f"rk_steps_{first}",
    )(table_rows, edge_cells, cells, *given, *pieces, *starts)
    return results[len(given) :]


def stretch_kernel(flow_ref, edge_ref, sides_ref, out_ref):
    _, rows, lanes = flow_ref.shape
    half = lanes // 2
    lane = lax.broadcasted_iota(jnp.int32, (8, lanes), 1)
    row = lax.broadcasted_iota(jnp.int32, (8, lanes), 0)
    sides = [sides_ref[part] for part in range(2)]
    south = [edge_ref[part, 0:1, :] for part in range(2)]
    north = [edge_ref[part, GROUP_ROWS : GROUP_ROWS + 1, :] for part in range(2)]
    tiles = rows // 8
    for at in range(tiles):
        start = at * 8
        index = jnp.where(lane < half, half + at, at)
        diff_lon, diff_lat = [], []
        for part in range(2):
            flow = flow_ref[part, start : start + 8, :]
            halo = jnp.take_along_axis(sides[part], index, axis=1, mode="promise_in_bounds")
            left = jnp.where(lane == 0, halo, pltpu.roll(flow, 1, 1))
            right = jnp.where(lane == lanes - 1, halo, pltpu.roll(flow, lanes - 1, 1))
            diff_lon.append((right - left) * 0.5)
            under = south[part] if at == 0 else flow_ref[part, start - 1 : start, :]
            over = north[part] if at == tiles - 1 else flow_ref[part, start + 8 : start + 9, :]
            below = jnp.where(row == 0, jnp.broadcast_to(under, flow.shape), pltpu.roll(flow, 1, 0))
            above = jnp.where(row == 7, jnp.broadcast_to(over, flow.shape), pltpu.roll(flow, 7, 0))
            diff_lat.append((above - below) * 0.5)
        out_ref[start : start + 8, :] = stretch_rate(diff_lon, diff_lat)


def stretch_rate(diff_lon, diff_lat):
    map_xx = 1.0 + diff_lon[0]
    map_xy = diff_lat[0]
    map_yx = diff_lon[1]
    map_yy = 1.0 + diff_lat[1]
    green_xx = map_xx * map_xx + map_yx * map_yx
    green_yy = map_xy * map_xy + map_yy * map_yy
    green_xy = map_xx * map_xy + map_yx * map_yy
    half_diff = 0.5 * (green_xx - green_yy)
    largest = 0.5 * (green_xx + green_yy) + jnp.sqrt(half_diff * half_diff + green_xy * green_xy)
    return 0.5 * jnp.log(largest)


def body(vel_base, vel_grad, route_dev, route_block, seed_cells):
    n_lon, n_lat = lax.axis_size("lon"), lax.axis_size("lat")
    num_steps, rows, lanes = seed_cells.shape
    blocks = vel_base.shape[3]
    step_rows = 6 * blocks
    shard = jnp.concatenate(
        [
            vel_base.reshape(num_steps, 2 * blocks, lanes),
            vel_grad.reshape(num_steps, 4 * blocks, lanes),
        ],
        axis=1,
    ).reshape(num_steps * step_rows, lanes)
    places = n_lon // 2
    owners = route_dev[0, 0, :, :, 0]
    wanted = route_block[0, 0]
    done = {}

    def gated(value, label):
        return after(value, *[done[name] for name in WAITS.get(label, ())])

    came = [shard]
    for apart in range(1, n_lat):
        done[f"z{apart}"] = swap(gated(shard, f"z{apart}"), "lat", (apart,))
        came.append(done[f"z{apart}"])
    even, odd = plane_masks(n_lon)
    held = [value[None] for value in came]
    for stage, masks in enumerate(zip(even, odd)):
        for apart in range(n_lat):
            label = f"r{apart}.{stage + 1}"
            sent = gated(held[apart], label)
            done[label] = swap(sent, "lon", masks)
            held[apart] = jnp.concatenate([sent, done[label]])
    def edge_of(row):
        value = jnp.stack([seed_cells[:, row, :], owners, wanted])
        return gated(value, "edge")

    south = lax.ppermute(edge_of(-1), "lat", [(i, i + 1) for i in range(n_lat - 1)])
    north = lax.ppermute(edge_of(0), "lat", [(i + 1, i) for i in range(n_lat - 1)])
    edge_cells = jnp.repeat(jnp.stack([south[0], north[0]], axis=1), GROUP_ROWS, axis=1)
    owners = jnp.concatenate([owners, south[1, :, -1:], north[1, :, :1]], axis=1)
    wanted = jnp.concatenate([wanted, south[2, :, -1:], north[2, :, :1]], axis=1)
    lat_index = lax.axis_index("lat")
    each = max(1, min(num_steps, TABLE_BYTES // (n_lon * n_lat * step_rows * lanes * 4)))
    spans = [(first, min(first + each, num_steps)) for first in range(0, num_steps, each)]
    slots = slot_of(owners, n_lat)
    local = jnp.arange(num_steps, dtype=jnp.int32)[:, None]
    rows_of = []
    for first, last in spans:
        row = (slots * (last - first) + local - first) * step_rows
        rows_of.append((row << (blocks - 1).bit_length()) + wanted)
    items = []
    for apart in range(n_lat):
        other = swap(gated(held[apart], f"c{apart}"), "lon", (1,))
        items += [(held[apart], 2 * apart * places), (other, (2 * apart + 1) * places)]
    state = None
    for (first, last), table_rows in zip(spans, rows_of):
        height = len(items) * places * (last - first) * step_rows
        scale = -0.5 / num_steps
        table = None
        for chosen in EARLY:
            chosen = [items[number] for number in chosen]
            table = run_widen(table, height, chosen, first, last, step_rows, scale)
        chosen = [items[number] for number in LATE]
        state = run_steps(
            first,
            last,
            scale,
            step_rows,
            height,
            table_rows,
            edge_cells,
            seed_cells,
            table,
            chosen,
            state,
        )
    flow, edge, out, sides = state
    inner = swap(sides, "lon", (1,))
    outer = lax.ppermute(
        sides, "lon", [(i, (i + (1 if i % 2 else -1)) % n_lon) for i in range(n_lon)]
    )
    south = jnp.where(lat_index == 0, flow[:, :1], edge[:, :1])
    north = jnp.where(lat_index == n_lat - 1, flow[:, -1:], edge[:, GROUP_ROWS : GROUP_ROWS + 1])
    edge = jnp.repeat(jnp.concatenate([south, north], axis=1), GROUP_ROWS, axis=1)
    lane = lax.broadcasted_iota(jnp.int32, sides.shape, 2)
    from_inner = (lane < lanes // 2) == (lax.axis_index("lon") % 2 == 0)
    sides = jnp.where(from_inner, inner, outer)
    vmem = pl.BlockSpec(memory_space=pltpu.VMEM)
    field = pl.pallas_call(
        stretch_kernel,
        out_shape=jax.ShapeDtypeStruct((rows, lanes), jnp.float32),
        in_specs=[vmem] * 3,
        out_specs=vmem,
        compiler_params=pltpu.CompilerParams(vmem_limit_bytes=16 << 20),
        name="stretch",
    )(flow, edge, sides)
    return (out, field)


def solution(mesh):
    in_specs = (
        P("lon", "lat", None, None, None, None),
        P("lon", "lat", None, None, None, None),
        P("lon", "lat", None, None, None),
        P("lon", "lat", None, None),
        P(None, "lat", "lon"),
    )
    out_specs = (P(None, "lat", "lon"), P("lat", "lon"))
    return jax.shard_map(body, mesh=mesh, in_specs=in_specs, out_specs=out_specs, check_vma=False)
```

```python
import functools

import jax
import jax.numpy as jnp
from jax import lax
from jax.experimental import pallas as pl
from jax.experimental.pallas import tpu as pltpu
from jax.sharding import PartitionSpec as P

GROUP_ROWS = 4
TABLE_BYTES = 13 << 20
EARLY = ((0, 1, 2, 3, 4, 5),)
LATE = (6, 7)
WAITS = {
    "z3": ("z1",),
    "edge": ("z1",),
    "r1.1": ("z1",),
    "r2.1": ("z1",),
    "r1.2": ("r0.2",),
    "r2.2": ("z2",),
    "c1": ("r2.1",),
    "c2": ("r3.1",),
}


def after(value, *earlier):
    return lax.optimization_barrier((value, *earlier))[0] if earlier else value


def swap(value, axis, masks):
    count = lax.axis_size(axis)
    pairs = [(i, i ^ masks[i % len(masks)]) for i in range(count)]
    return lax.ppermute(value, axis, pairs)


def plane_masks(n_lon):
    bits = []
    mask = 2
    while mask < n_lon:
        bits.append(mask)
        mask *= 2
    return bits, bits[::-1]


def slot_of(owners, n_lat):
    lon, lat = lax.axis_index("lon"), lax.axis_index("lat")
    even, odd = plane_masks(lax.axis_size("lon"))
    places = 1 << len(even)
    owner_lon, owner_lat = owners // n_lat, owners % n_lat
    apart = owner_lat ^ lat
    foreign = (owner_lon ^ lon) & 1
    base = lon ^ foreign
    diff = owner_lon ^ base
    place = jnp.zeros_like(owners)
    for position, (even_mask, odd_mask) in enumerate(zip(even, odd)):
        mask = jnp.where((base & 1) == 0, even_mask, odd_mask)
        place = place + jnp.where((diff & mask) != 0, 1 << position, 0)
    return (apart * 2 + foreign) * places + place


def advance(along_x, along_y, coeffs):
    vel_x, vel_y, xx, xy, yx, yy = coeffs
    half_x = vel_x + xx * along_x + xy * along_y
    half_y = vel_y + yx * along_x + yy * along_y
    full_x = half_x + half_x
    full_y = half_y + half_y
    third_x = full_x + (xx * half_x + xy * half_y)
    third_y = full_y + (yx * half_x + yy * half_y)
    ratio = 2.0 / 3.0
    second_x = full_x + ratio * (xx * third_x + xy * third_y)
    second_y = full_y + ratio * (yx * third_x + yy * third_y)
    new_x = along_x + (full_x + (xx * second_x + xy * second_y))
    new_y = along_y + (full_y + (yx * second_x + yy * second_y))
    return new_x, new_y


def widen_pieces(table, slots, pieces, first, steps, step_rows, scale):
    for slot, piece in zip(slots, pieces):

        def widen(part, carry, slot=slot, piece=piece):
            place, step = part // steps, part % steps
            source = pl.multiple_of((first + step) * step_rows, step_rows)
            row = pl.multiple_of((slot * steps + part) * step_rows, step_rows)
            values = piece[place, pl.ds(source, step_rows), :].astype(jnp.float32) * scale
            table[pl.ds(row, step_rows), :] = values
            return carry

        lax.fori_loop(0, piece.shape[0] * steps, widen, 0, unroll=8)


def widen_kernel(slots, has_table, first, steps, step_rows, scale, *refs):
    pieces = refs[1:-1] if has_table else refs[:-1]
    widen_pieces(refs[-1], slots, pieces, first, steps, step_rows, scale)


def run_widen(table, height, items, first, last, step_rows, scale):
    pieces = [item[0] for item in items]
    slots = tuple(item[1] for item in items)
    lanes = pieces[0].shape[-1]
    vmem = pl.BlockSpec(memory_space=pltpu.VMEM)
    given = [table] if table is not None else []
    return pl.pallas_call(
        functools.partial(
            widen_kernel, slots, table is not None, first, last - first, step_rows, scale
        ),
        out_shape=jax.ShapeDtypeStruct((height, lanes), jnp.float32),
        in_specs=[vmem] * len(given + pieces),
        out_specs=vmem,
        input_output_aliases={0: 0} if given else {},
        cost_estimate=pl.CostEstimate(flops=0, bytes_accessed=8 << 20, transcendentals=0),
        compiler_params=pltpu.CompilerParams(vmem_limit_bytes=4 << 20),
        name=f"widen_{first}",
    )(*given, *pieces)


def steps_kernel(first, scale, step_rows, slots, has_table, has_start, last, unroll, *refs):
    count = len(slots)
    rows_ref, edge_ref, cells_hbm = refs[:3]
    given = refs[4:] if has_table else refs[3:]
    pieces = given[:count]
    start_ref, start_edge = given[count : count + 2] if has_start else (None, None)
    rest = given[count + 2 :] if has_start else given[count:]
    table, rest = (rest[0], rest[1:]) if has_table else (rest[-4], rest)
    flow_ref, out_edge = rest[:2]
    out_hbm, out_sides = rest[2:4] if last else (None, None)
    cells_ref, arrived, written = rest[-3:]
    steps, rows, lanes = cells_ref.shape
    fetch = pltpu.make_async_copy(cells_hbm.at[pl.ds(first, steps)], cells_ref, arrived)
    fetch.start()
    widen_pieces(table, slots, pieces, first, steps, step_rows, scale)
    fetch.wait()
    upper = lax.broadcasted_iota(jnp.int32, (8, lanes), 0) < GROUP_ROWS
    lane = lax.broadcasted_iota(jnp.int32, (8, lanes), 1)
    zero = jnp.zeros((8, lanes), jnp.float32)
    groups = rows // GROUP_ROWS
    blocks = step_rows // 6
    shift = (blocks - 1).bit_length()

    def begin_at(ref, row):
        return (ref[0, pl.ds(row, 8), :], ref[1, pl.ds(row, 8), :]) if has_start else (zero, zero)

    def tile(one, two, indices, along_x, along_y):
        for step in range(steps):
            index = indices(step)
            places = []
            for which in (one, two):
                code = rows_ref[first + step, which]
                block = code & ((1 << shift) - 1)
                start = lax.shift_right_logical(code, shift)
                places.append((start + 2 * block, start + 2 * blocks + 4 * block))
            sources = [
                (places[0][kind] + k, places[1][kind] + k)
                for kind, number in ((0, 2), (1, 4))
                for k in range(number)
            ]
            coeffs = []
            for above, below in sources:
                values = jnp.where(
                    upper,
                    jnp.broadcast_to(table[pl.ds(above, 1), :], (8, lanes)),
                    jnp.broadcast_to(table[pl.ds(below, 1), :], (8, lanes)),
                )
                coeffs.append(
                    jnp.take_along_axis(values, index, axis=1, mode="promise_in_bounds")
                )
            along_x, along_y = advance(along_x, along_y, coeffs)
        return along_x, along_y

    block = 8 * unroll

    def send(number):
        part = pl.ds(pl.multiple_of(number * block, block), block)
        return pltpu.make_async_copy(flow_ref.at[:, part], out_hbm.at[:, part], written.at[number])

    def tiles(number, carry):
        for inner in range(unroll):
            at = number * unroll + inner
            row = pl.multiple_of(at * 8, 8)
            start = begin_at(start_ref, row)
            end = tile(2 * at, 2 * at + 1, lambda step: cells_ref[step, pl.ds(row, 8), :], *start)
            flow_ref[0, pl.ds(row, 8), :], flow_ref[1, pl.ds(row, 8), :] = end
        if last:
            send(number).start()
        return carry

    lax.fori_loop(0, rows // block, tiles, 0)
    start = begin_at(start_edge, 0)
    end = tile(groups, groups + 1, lambda step: edge_ref[first + step], *start)
    out_edge[0], out_edge[1] = end
    if not last:
        return
    half = lanes // 2
    ends = jnp.where(lane < half, 0, lanes - 1)
    for part in range(2):
        sides = [zero] * 4
        for at in range(rows // 8):
            value = flow_ref[part, at * 8 : at * 8 + 8, :]
            value = jnp.take_along_axis(value, ends, axis=1, mode="promise_in_bounds")
            sides[at % 4] = jnp.where((lane & (half - 1)) == at, value, sides[at % 4])
        out_sides[part] = (sides[0] + sides[1]) + (sides[2] + sides[3])
    for number in range(rows // block):
        send(number).wait()


def run_steps(
    first, last, scale, step_rows, height, table_rows, edge_cells, cells, table, items, start
):
    num_steps, rows, lanes = cells.shape
    steps = last - first
    pieces = [item[0] for item in items]
    slots = tuple(item[1] for item in items)
    vmem = pl.BlockSpec(memory_space=pltpu.VMEM)
    smem = pl.BlockSpec(memory_space=pltpu.SMEM)
    hbm = pl.BlockSpec(memory_space=pltpu.HBM)
    need = steps * rows * lanes * 4
    small = jax.ShapeDtypeStruct((2, 8, lanes), jnp.float32)
    whole = jax.ShapeDtypeStruct((2, rows, lanes), jnp.float32)
    final = last == num_steps
    starts = list(start) if first else []
    given = [table] if table is not None else []
    shape = jax.ShapeDtypeStruct((height, lanes), jnp.float32)
    need += 0 if given else height * lanes * 4
    unroll = 16
    results = pl.pallas_call(
        functools.partial(
            steps_kernel, first, scale, step_rows, slots, len(given) > 0, first > 0, final, unroll
        ),
        out_shape=(shape,) * len(given) + (whole, small) + ((whole, small) if final else ()),
        in_specs=[smem, vmem, hbm] + [vmem] * len(given + pieces + starts),
        out_specs=(vmem,) * len(given) + (vmem, vmem) + ((hbm, vmem) if final else ()),
        input_output_aliases={3: 0} if given else {},
        scratch_shapes=([] if given else [pltpu.VMEM(shape.shape, shape.dtype)])
        + [
            pltpu.VMEM((steps, rows, lanes), jnp.int32),
            pltpu.SemaphoreType.DMA(()),
            pltpu.SemaphoreType.DMA((rows // 8 // unroll,)),
        ],
        cost_estimate=pl.CostEstimate(
            flops=40 * steps * rows * lanes, bytes_accessed=16 << 20, transcendentals=0
        ),
        compiler_params=pltpu.CompilerParams(vmem_limit_bytes=need + (4 << 20)),
        name=f"rk_steps_{first}",
    )(table_rows, edge_cells, cells, *given, *pieces, *starts)
    return results[len(given) :]


def stretch_kernel(flow_ref, edge_ref, sides_ref, out_ref):
    _, rows, lanes = flow_ref.shape
    half = lanes // 2
    lane = lax.broadcasted_iota(jnp.int32, (8, lanes), 1)
    row = lax.broadcasted_iota(jnp.int32, (8, lanes), 0)
    sides = [sides_ref[part] for part in range(2)]
    south = [edge_ref[part, 0:1, :] for part in range(2)]
    north = [edge_ref[part, GROUP_ROWS : GROUP_ROWS + 1, :] for part in range(2)]
    tiles = rows // 8
    for at in range(tiles):
        start = at * 8
        index = jnp.where(lane < half, half + at, at)
        diff_lon, diff_lat = [], []
        for part in range(2):
            flow = flow_ref[part, start : start + 8, :]
            halo = jnp.take_along_axis(sides[part], index, axis=1, mode="promise_in_bounds")
            left = jnp.where(lane == 0, halo, pltpu.roll(flow, 1, 1))
            right = jnp.where(lane == lanes - 1, halo, pltpu.roll(flow, lanes - 1, 1))
            diff_lon.append((right - left) * 0.5)
            under = south[part] if at == 0 else flow_ref[part, start - 1 : start, :]
            over = north[part] if at == tiles - 1 else flow_ref[part, start + 8 : start + 9, :]
            below = jnp.where(row == 0, jnp.broadcast_to(under, flow.shape), pltpu.roll(flow, 1, 0))
            above = jnp.where(row == 7, jnp.broadcast_to(over, flow.shape), pltpu.roll(flow, 7, 0))
            diff_lat.append((above - below) * 0.5)
        out_ref[start : start + 8, :] = stretch_rate(diff_lon, diff_lat)


def stretch_rate(diff_lon, diff_lat):
    map_xx = 1.0 + diff_lon[0]
    map_xy = diff_lat[0]
    map_yx = diff_lon[1]
    map_yy = 1.0 + diff_lat[1]
    green_xx = map_xx * map_xx + map_yx * map_yx
    green_yy = map_xy * map_xy + map_yy * map_yy
    green_xy = map_xx * map_xy + map_yx * map_yy
    half_diff = 0.5 * (green_xx - green_yy)
    largest = 0.5 * (green_xx + green_yy) + jnp.sqrt(half_diff * half_diff + green_xy * green_xy)
    return 0.5 * jnp.log(largest)


def body(vel_base, vel_grad, route_dev, route_block, seed_cells):
    n_lon, n_lat = lax.axis_size("lon"), lax.axis_size("lat")
    num_steps, rows, lanes = seed_cells.shape
    blocks = vel_base.shape[3]
    step_rows = 6 * blocks
    shard = jnp.concatenate(
        [
            vel_base.reshape(num_steps, 2 * blocks, lanes),
            vel_grad.reshape(num_steps, 4 * blocks, lanes),
        ],
        axis=1,
    ).reshape(num_steps * step_rows, lanes)
    places = n_lon // 2
    owners = route_dev[0, 0, :, :, 0]
    wanted = route_block[0, 0]
    done = {}

    def gated(value, label):
        return after(value, *[done[name] for name in WAITS.get(label, ())])

    came = [shard]
    for apart in range(1, n_lat):
        done[f"z{apart}"] = swap(gated(shard, f"z{apart}"), "lat", (apart,))
        came.append(done[f"z{apart}"])
    even, odd = plane_masks(n_lon)
    held = [value[None] for value in came]
    for stage, masks in enumerate(zip(even, odd)):
        for apart in range(n_lat):
            label = f"r{apart}.{stage + 1}"
            sent = gated(held[apart], label)
            done[label] = swap(sent, "lon", masks)
            held[apart] = jnp.concatenate([sent, done[label]])
    def edge_of(row):
        value = jnp.stack([seed_cells[:, row, :], owners, wanted])
        return gated(value, "edge")

    south = lax.ppermute(edge_of(-1), "lat", [(i, i + 1) for i in range(n_lat - 1)])
    north = lax.ppermute(edge_of(0), "lat", [(i + 1, i) for i in range(n_lat - 1)])
    edge_cells = jnp.repeat(jnp.stack([south[0], north[0]], axis=1), GROUP_ROWS, axis=1)
    owners = jnp.concatenate([owners, south[1, :, -1:], north[1, :, :1]], axis=1)
    wanted = jnp.concatenate([wanted, south[2, :, -1:], north[2, :, :1]], axis=1)
    lat_index = lax.axis_index("lat")
    each = max(1, min(num_steps, TABLE_BYTES // (n_lon * n_lat * step_rows * lanes * 4)))
    spans = [(first, min(first + each, num_steps)) for first in range(0, num_steps, each)]
    slots = slot_of(owners, n_lat)
    local = jnp.arange(num_steps, dtype=jnp.int32)[:, None]
    rows_of = []
    for first, last in spans:
        row = (slots * (last - first) + local - first) * step_rows
        rows_of.append((row << (blocks - 1).bit_length()) + wanted)
    items = []
    for apart in range(n_lat):
        other = swap(gated(held[apart], f"c{apart}"), "lon", (1,))
        items += [(held[apart], 2 * apart * places), (other, (2 * apart + 1) * places)]
    state = None
    for (first, last), table_rows in zip(spans, rows_of):
        height = len(items) * places * (last - first) * step_rows
        scale = -0.5 / num_steps
        table = None
        for chosen in EARLY:
            chosen = [items[number] for number in chosen]
            table = run_widen(table, height, chosen, first, last, step_rows, scale)
        chosen = [items[number] for number in LATE]
        state = run_steps(
            first,
            last,
            scale,
            step_rows,
            height,
            table_rows,
            edge_cells,
            seed_cells,
            table,
            chosen,
            state,
        )
    flow, edge, out, sides = state
    outer = lax.ppermute(
        sides, "lon", [(i, (i + (1 if i % 2 else -1)) % n_lon) for i in range(n_lon)]
    )
    south = jnp.where(lat_index == 0, flow[:, :1], edge[:, :1])
    north = jnp.where(lat_index == n_lat - 1, flow[:, -1:], edge[:, GROUP_ROWS : GROUP_ROWS + 1])
    edge = jnp.repeat(jnp.concatenate([south, north], axis=1), GROUP_ROWS, axis=1)
    inner = swap(after(sides, edge), "lon", (1,))
    lane = lax.broadcasted_iota(jnp.int32, sides.shape, 2)
    from_inner = (lane < lanes // 2) == (lax.axis_index("lon") % 2 == 0)
    sides = jnp.where(from_inner, inner, outer)
    vmem = pl.BlockSpec(memory_space=pltpu.VMEM)
    field = pl.pallas_call(
        stretch_kernel,
        out_shape=jax.ShapeDtypeStruct((rows, lanes), jnp.float32),
        in_specs=[vmem] * 3,
        out_specs=vmem,
        compiler_params=pltpu.CompilerParams(vmem_limit_bytes=16 << 20),
        name="stretch",
    )(flow, edge, sides)
    return (out, field)


def solution(mesh):
    in_specs = (
        P("lon", "lat", None, None, None, None),
        P("lon", "lat", None, None, None, None),
        P("lon", "lat", None, None, None),
        P("lon", "lat", None, None),
        P(None, "lat", "lon"),
    )
    out_specs = (P(None, "lat", "lon"), P("lat", "lon"))
    return jax.shard_map(body, mesh=mesh, in_specs=in_specs, out_specs=out_specs, check_vma=False)
```
